32 devices in a mesh: slot: 4 (over y, x), seq: 8 (over z, core).
Axes of the slice: x: 2, y: 2, z: 4, core: 2. Of those that a mesh axis runs over, the one named last changes fastest.
Arguments:
- rows_in: bfloat16 [4, 2048, 2048], P('slot', 'seq'), may hold values from -6 to 6
- lengths: int32 [4], P('slot'), may hold values from 64 to 2048, as said below
- norm1_gain: bfloat16 [2048], P('seq'), may hold values from 0.5 to 1.5
- w_query: bfloat16 [2048, 2048], P('seq'), may hold values from -0.125 to 0.125
- w_key: bfloat16 [2048, 128], P('seq'), may hold values from -0.125 to 0.125
- w_value: bfloat16 [2048, 128], P('seq'), may hold values from -0.125 to 0.125
- w_out: bfloat16 [2048, 2048], P('seq'), may hold values from -0.5 to 0.5
- norm2_gain: bfloat16 [2048], P('seq'), may hold values from 0.5 to 1.5
- w_gate: bfloat16 [2048, 5632], P('seq'), may hold values from -0.125 to 0.125
- w_up: bfloat16 [2048, 5632], P('seq'), may hold values from -0.125 to 0.125
- w_down: bfloat16 [5632, 2048], P('seq'), may hold values from -0.078125 to 0.078125
- rows_cot: bfloat16 [4, 2048, 2048], P('slot', 'seq'), may hold values from -6 to 6
- kv_cot: bfloat16 [4, 2048, 256], P('slot', 'seq'), may hold values from -6 to 6
Outputs:
- rows: bfloat16 [4, 2048, 2048], P('slot', 'seq')
- shared_kv: bfloat16 [4, 2048, 256], P('slot', 'seq')
- input_grad: bfloat16 [4, 2048, 2048], P('slot', 'seq')
- norm1_gain_grad: float32 [2048], P('seq')
- w_query_grad: float32 [2048, 2048], P('seq')
- w_key_grad: float32 [2048, 128], P('seq')
- w_value_grad: float32 [2048, 128], P('seq')
- w_out_grad: float32 [2048, 2048], P('seq')
- norm2_gain_grad: float32 [2048], P('seq')
- w_gate_grad: float32 [2048, 5632], P('seq')
- w_up_grad: float32 [2048, 5632], P('seq')
- w_down_grad: float32 [5632, 2048], P('seq')
The draws below stay inside these ranges and needn't reach their ends.
Inputs may be any that keep to these rules, and one draw needn't show every extreme that they name: `lengths`: one slot, drawn from the seed, has length 2048; the others lie between 64 and 2048.
All inputs are finite; a program needn't handle non-finite values.
Results may differ from the reference program's by a relative error of at most 0.02.
Values may be sent and summed in bfloat16 or wider, within the bound.
No kernel may reach another device: no remote copies, remote signals or barrier semaphores. Data moves between devices by JAX's collectives and lax.ppermute only.
A program may use at most 384 MiB of HBM per device.

```python
import jax
import jax.numpy as jnp
from jax import lax

D = 2048
H = 16
HD = 128
FF = 5632
WINDOW = 512
MIN_LEN = 64
TOK_DEV = 256
SLOTS = 4
LEN = 2048
N_SEQ = 8


def draw_lengths(key, part):
    key = jax.random.fold_in(key, 7)
    pair_key, pick_key = jax.random.split(key)
    pair_draw = jax.random.randint(pair_key, (SLOTS, 2), MIN_LEN, LEN + 1)
    longer = jnp.max(pair_draw, axis=1)
    chosen = jax.random.randint(pick_key, (), 0, SLOTS)
    return jnp.where(jnp.arange(SLOTS) == chosen, LEN, longer).astype(jnp.int32)


def block_levels(own_key, shape, pieces, least, largest):
    def one(dim, blocks):
        draws = jax.random.uniform(jax.random.fold_in(jax.random.fold_in(own_key, 6), dim), (blocks,), jnp.float32, least / len(pieces), largest / len(pieces))
        return jnp.repeat(jnp.exp(draws), shape[dim] // blocks).reshape((-1,) + (1,) * (len(shape) - dim - 1))

    factor_of = one(*pieces[0])
    for cut in pieces[1:]:
        factor_of = factor_of * one(*cut)
    return factor_of


def normal_values(stream_key, shape, deviation, most, shards=(), kind=jnp.bfloat16):
    values = deviation * jax.random.normal(stream_key, shape, jnp.float32)
    if shards:
        values = values * block_levels(stream_key, shape, shards, -0.22, 0.18)
    return jnp.clip(values, -most, most).astype(kind)


def setup_inputs(seed: int = 0) -> dict:
    streams_of = jax.random.split(jax.random.key(seed), 14)
    return {
        "rows_in": normal_values(streams_of[0], (SLOTS, LEN, D), 1.0, 6.0, ((0, 4), (1, 8))),
        "lengths": draw_lengths(jax.random.fold_in(streams_of[13], 71), 0),
        "norm1_gain": jnp.clip(1.0 + 0.1 * jax.random.normal(streams_of[2], (D,), jnp.float32), 0.5, 1.5).astype(jnp.bfloat16),
        "w_query": normal_values(streams_of[3], (D, H * HD), D ** -0.5, 0.125, ((0, 8),)),
        "w_key": normal_values(streams_of[4], (D, HD), D ** -0.5, 0.125, ((0, 8),)),
        "w_value": normal_values(streams_of[5], (D, HD), D ** -0.5, 0.125, ((0, 8),)),
        "w_out": normal_values(streams_of[6], (H * HD, D), (H * HD // 16) ** -0.5, 0.5, ((0, 8),)),
        "norm2_gain": jnp.clip(1.0 + 0.1 * jax.random.normal(streams_of[7], (D,), jnp.float32), 0.5, 1.5).astype(jnp.bfloat16),
        "w_gate": normal_values(streams_of[8], (D, FF), D ** -0.5, 0.125, ((0, 8),)),
        "w_up": normal_values(streams_of[9], (D, FF), D ** -0.5, 0.125, ((0, 8),)),
        "w_down": normal_values(streams_of[10], (FF, D), FF ** -0.5, 0.078125, ((0, 8),)),
        "rows_cot": normal_values(streams_of[11], (SLOTS, LEN, D), 1.0, 6.0, ((0, 4), (1, 8))),
        "kv_cot": normal_values(streams_of[12], (SLOTS, LEN, 2 * HD), 1.0, 6.0, ((0, 4), (1, 8))),
    }


EPSILON = 1e-05
THETA = 10000.0
NEGATIVE = -1e+30
HIGHEST_PRECISION = lax.Precision.HIGHEST

@jax.custom_vjp
def low(v):
    return lax.optimization_barrier(v.astype(jnp.bfloat16)).astype(jnp.float32)

@jax.custom_vjp
def low_back(v):
    return v

def low_keep(v):
    return (low(v), None)

def low_pass(kept, grad):
    return (grad,)

def back_keep(v):
    return (v, None)

def back_low(kept, grad):
    return (low(grad),)
low.defvjp(low_keep, low_pass)
low_back.defvjp(back_keep, back_low)

def rope_tables(positions, head_width):
    half_width = head_width // 2
    exponent = jnp.arange(half_width, dtype=jnp.float32) * (2.0 / head_width)
    frequency = THETA ** (-exponent)
    angles = positions.astype(jnp.float32)[:, None] * frequency[None, :]
    return (jnp.cos(angles), jnp.sin(angles))

def rotate(values, cosine_table, sine_table):
    half_width = values.shape[-1] // 2
    first_half = values[..., :half_width]
    second_half = values[..., half_width:]
    return jnp.concatenate([first_half * cosine_table - second_half * sine_table, second_half * cosine_table + first_half * sine_table], axis=-1)

def rms_scale(values):
    return lax.rsqrt(lax.optimization_barrier(jnp.mean(values * values, axis=-1, keepdims=True)) + EPSILON)

def window_mask(query_pos, key_pos, length):
    distance = query_pos[:, None] - key_pos[None, :]
    return (key_pos[None, :] >= 0) & (key_pos[None, :] < length) & (distance >= 0) & (distance < WINDOW) & (query_pos[:, None] < length)

def attend_block(block_index, queries, key_table, length):
    first_row = block_index * TOK_DEV
    query_block = lax.dynamic_slice_in_dim(queries, first_row, TOK_DEV, 0)
    key_block = lax.dynamic_slice_in_dim(key_table, first_row, WINDOW + TOK_DEV, 0)
    key_part = key_block[:, :HD]
    value_part = key_block[:, HD:]
    raw_scores = jnp.einsum('chd,kd->chk', query_block, key_part, precision=HIGHEST_PRECISION) * HD ** (-0.5)
    raw_scores = low_back(raw_scores)
    query_pos = first_row + jnp.arange(TOK_DEV, dtype=jnp.int32)
    key_pos = first_row - WINDOW + jnp.arange(WINDOW + TOK_DEV, dtype=jnp.int32)
    allowed = window_mask(query_pos, key_pos, length)[:, None, :]
    masked = jnp.where(allowed, raw_scores, NEGATIVE)
    row_max = lax.optimization_barrier(jnp.max(masked, axis=-1, keepdims=True))
    exponent_rows = jnp.exp(masked - row_max) * allowed.astype(jnp.float32)
    row_sum = lax.optimization_barrier(jnp.sum(exponent_rows, axis=-1, keepdims=True))
    row_valid = (query_pos < length)[:, None, None]
    row_denom = jnp.where(row_valid, row_sum, 1.0)
    prob_rows = low(exponent_rows / row_denom)
    return jnp.einsum('chk,kd->chd', prob_rows, value_part, precision=HIGHEST_PRECISION)

def layer_slot(params, slot_rows, length):
    norm1_gain, w_query, w_key, w_value, w_out, norm2_gain, w_gate, w_up, w_down = params
    positions = jnp.arange(LEN, dtype=jnp.int32)
    row_valid = (positions < length).astype(jnp.float32)[:, None]
    normed = low(slot_rows * rms_scale(slot_rows) * norm1_gain)
    cosine_table, sine_table = rope_tables(positions, HD)
    query_pre = low_back(jnp.dot(normed, w_query, precision=HIGHEST_PRECISION))
    key_pre = low_back(jnp.dot(normed, w_key, precision=HIGHEST_PRECISION))
    value_rows = low(low_back(jnp.dot(normed, w_value, precision=HIGHEST_PRECISION)))
    queries = low(rotate(query_pre.reshape(LEN, H, HD), cosine_table[:, None, :], sine_table[:, None, :]))
    key_rows = low(rotate(key_pre, cosine_table, sine_table))
    shared = jnp.concatenate([key_rows, value_rows], axis=1) * row_valid
    key_table = jnp.concatenate([jnp.zeros((WINDOW, 2 * HD), jnp.float32), shared], axis=0)

    def block_fn(block_index):
        return attend_block(block_index, queries, key_table, length)
    attended = lax.map(jax.checkpoint(block_fn), jnp.arange(N_SEQ, dtype=jnp.int32))
    attended = low_back(low(attended.reshape(LEN, H * HD)))
    branch = low_back(jnp.dot(attended, w_out, precision=HIGHEST_PRECISION))
    middle = slot_rows + branch
    normed_two = low(middle * rms_scale(middle) * norm2_gain)
    gate_out = low_back(jnp.dot(normed_two, w_gate, precision=HIGHEST_PRECISION))
    up_out = low_back(jnp.dot(normed_two, w_up, precision=HIGHEST_PRECISION))
    hidden = low(jax.nn.silu(gate_out) * up_out)
    result = middle + jnp.dot(hidden, w_down, precision=HIGHEST_PRECISION) * row_valid
    return (result, shared)

def reference(rows_in, lengths, norm1_gain, w_query, w_key, w_value, w_out, norm2_gain, w_gate, w_up, w_down, rows_cot, kv_cot):
    params = tuple((weight.astype(jnp.float32) for weight in (norm1_gain, w_query, w_key, w_value, w_out, norm2_gain, w_gate, w_up, w_down)))

    def forward(params, rows_all):

        def slot_step(carried, slot_item):
            slot_rows, length = slot_item
            return (carried, jax.checkpoint(layer_slot)(params, slot_rows, length))
        _, outputs = lax.scan(slot_step, jnp.zeros((), jnp.float32), (rows_all, lengths))
        return outputs
    outputs, pullback = jax.vjp(forward, params, rows_in.astype(jnp.float32))
    param_grads, row_grads = pullback((rows_cot.astype(jnp.float32), kv_cot.astype(jnp.float32)))
    return (outputs[0].astype(jnp.bfloat16), outputs[1].astype(jnp.bfloat16), row_grads.astype(jnp.bfloat16), param_grads[0], param_grads[1], param_grads[2], param_grads[3], param_grads[4], param_grads[5], param_grads[6], param_grads[7], param_grads[8])
```

```python
import jax
import jax.numpy as jnp
from jax import lax
from jax.sharding import PartitionSpec as P

WINDOW = 512


EPSILON = 1e-05
THETA = 10000.0
NEGATIVE = -1e30
BF = jnp.bfloat16
F32 = jnp.float32


def swap(block, axis, mask):
    return lax.ppermute(block, axis, [(i, i ^ mask) for i in range(lax.axis_size(axis))])


def gather_slot(block):
    count = lax.axis_size("slot")
    if count != 4:
        return [block] + [swap(block, "slot", j) for j in range(1, count)]
    half = block.shape[0] // 2
    one = swap(block, "slot", 1)
    two = swap(block, "slot", 2)
    low = swap(one[:half], "slot", 2)
    high = swap(two[half:], "slot", 1)
    return [block, one, two, jnp.concatenate([low, high], axis=0)]


def scatter_slot(blocks):
    count = lax.axis_size("slot")
    own = blocks[0].astype(F32)
    if count != 4:
        for j in range(1, count):
            own = own + swap(blocks[j], "slot", j).astype(F32)
        return own
    half = blocks[0].shape[0] // 2
    low = swap(blocks[3][:half], "slot", 2)
    high = swap(blocks[3][half:], "slot", 1)
    one_high = swap(blocks[1][half:], "slot", 1)
    two_low = swap(blocks[2][:half], "slot", 2)
    one_low = swap((blocks[1][:half].astype(F32) + low.astype(F32)).astype(BF), "slot", 1)
    two_high = swap((blocks[2][half:].astype(F32) + high.astype(F32)).astype(BF), "slot", 2)
    first = jnp.concatenate([one_low, one_high], axis=0).astype(F32)
    second = jnp.concatenate([two_low, two_high], axis=0).astype(F32)
    return own + first + second


def trade_slot(blocks):
    return [blocks[0]] + [swap(blocks[j], "slot", j) for j in range(1, len(blocks))]


def gather_line(block):
    count = lax.axis_size("seq")
    if count != 8:
        return [block] + [swap(block, "seq", j) for j in range(2, count, 2)]
    one = swap(block, "seq", 2)
    three = swap(block, "seq", 6)
    two = swap(three, "seq", 2)
    return [block, one, two, three]


def both_cores(blocks):
    out = []
    for block in blocks:
        out += [block, swap(block, "seq", 1)]
    return out


def scatter_seq(blocks):
    count = lax.axis_size("seq")
    line = []
    for j in range(0, count, 2):
        line.append(blocks[j].astype(F32) + swap(blocks[j + 1], "seq", 1).astype(F32))
    if count != 8:
        own = line[0]
        for k in range(1, count // 2):
            own = own + swap(line[k].astype(BF), "seq", 2 * k).astype(F32)
        return own
    own, one, two, three = line
    passed = swap(two.astype(BF), "seq", 2)
    near = swap(one.astype(BF), "seq", 2)
    far = swap((three + passed.astype(F32)).astype(BF), "seq", 6)
    return own + near.astype(F32) + far.astype(F32)


def xor_blocks(values, index, count, axis):
    width = values.shape[axis] // count
    return jnp.concatenate(
        [lax.dynamic_slice_in_dim(values, (index ^ j) * width, width, axis) for j in range(count)],
        axis=axis,
    )


def shifted(block, axis, distance):
    devices = range(lax.axis_size(axis))
    route = [(i - distance, i) for i in devices if i - distance in devices]
    return lax.ppermute(block, axis, route)


def rope_tables(positions, head_width):
    half_width = head_width // 2
    exponent = jnp.arange(half_width, dtype=jnp.float32) * (2.0 / head_width)
    frequency = THETA ** (-exponent)
    angles = positions.astype(jnp.float32)[:, None] * frequency[None, :]
    return (jnp.cos(angles), jnp.sin(angles))


def rotate(values, cosine_table, sine_table):
    half_width = values.shape[-1] // 2
    first_half = values[..., :half_width]
    second_half = values[..., half_width:]
    return jnp.concatenate(
        [
            first_half * cosine_table - second_half * sine_table,
            second_half * cosine_table + first_half * sine_table,
        ],
        axis=-1,
    )


def rms_scale(values):
    return lax.rsqrt(jnp.mean(values * values, axis=-1, keepdims=True) + EPSILON)


def window_mask(query_pos, key_pos, length):
    distance = query_pos[:, None] - key_pos[None, :]
    return (
        (key_pos[None, :] >= 0)
        & (key_pos[None, :] < length)
        & (distance >= 0)
        & (distance < WINDOW)
        & (query_pos[:, None] < length)
    )


def norm_back(grad_normed, unit_rows, scale_rows, gain_row):
    scaled = grad_normed * gain_row.astype(jnp.float32)
    return scale_rows * (scaled - unit_rows * jnp.mean(scaled * unit_rows, axis=-1, keepdims=True))


def dot(left, right):
    return jnp.dot(left, right, preferred_element_type=F32)


def dot_nt(left, right):
    return lax.dot_general(left, right, (((1,), (1,)), ((), ())), preferred_element_type=F32)


def dot_tn(left, right):
    return lax.dot_general(left, right, (((0,), (0,)), ((), ())), preferred_element_type=F32)


def shards(
    rows_in,
    lengths,
    norm1_gain,
    w_query,
    w_key,
    w_value,
    w_out,
    norm2_gain,
    w_gate,
    w_up,
    w_down,
    rows_cot,
    kv_cot,
):
    slots = lax.axis_size("slot")
    seqs = lax.axis_size("seq")
    slot = lax.axis_index("slot")
    seq = lax.axis_index("seq")
    tok_count = rows_in.shape[1]
    model = rows_in.shape[2]
    head_width = w_key.shape[1]
    head_count = w_query.shape[1] // head_width
    hop_count = WINDOW // tok_count
    key_count = WINDOW + tok_count
    scaling = head_width ** (-0.5)
    rows_dev = w_query.shape[0]
    cols_slot = w_query.shape[1] // slots
    out_slot = w_out.shape[1] // slots
    hidden_all = w_gate.shape[1]
    piece = hidden_all // (slots * seqs)
    hidden_slot = piece * seqs
    kv_width = 2 * head_width

    gains = jnp.stack([norm1_gain, norm2_gain], axis=0)
    pack = jnp.concatenate(
        [lax.dynamic_slice_in_dim(w_query, slot * cols_slot, cols_slot, 1), w_key, w_value], axis=1
    )
    gains = jnp.pad(gains, ((0, 14), (0, pack.shape[1] - rows_dev)))
    pack_line = gather_line(jnp.concatenate([pack, gains], axis=0))
    out_line = gather_line(lax.dynamic_slice_in_dim(w_out, slot * out_slot, out_slot, 1))

    def spread(line):
        cut = len(line) // 2
        parts = []
        for group in (line[:cut], line[cut:]):
            got = gather_slot(jnp.concatenate(group, axis=0))
            parts.append(jnp.concatenate(got, axis=1))
        whole = jnp.concatenate(parts, axis=0)
        other = swap(whole, "seq", 1)
        mine = whole.reshape(len(line), rows_dev, -1)
        theirs = other.reshape(len(line), rows_dev, -1)
        return jnp.stack([mine, theirs], axis=1).reshape(2 * len(line) * rows_dev, -1)

    query_w = spread([block[:rows_dev, :cols_slot] for block in pack_line])
    rest = both_cores([block[:, cols_slot:] for block in pack_line])
    kv_w = jnp.concatenate([block[:rows_dev] for block in rest], axis=0)
    gain_rows = both_cores([block[rows_dev:, :rows_dev] for block in pack_line])
    gain_x = jnp.concatenate([block[:2] for block in gain_rows], axis=1)
    gain_both = xor_blocks(gain_x, seq, seqs, 1)
    gain_one, gain_two = gain_both[0], gain_both[1]
    out_w = spread(out_line)

    def share(weight):
        cut = weight.reshape(rows_dev, seqs, slots, piece)
        return lax.dynamic_index_in_dim(cut, slot, 2, keepdims=False).reshape(rows_dev, hidden_slot)

    gu_line = gather_line(jnp.concatenate([share(w_gate), share(w_up)], axis=1))
    down_line = gather_line(lax.dynamic_slice_in_dim(w_down, slot * piece, piece, 0))
    gu_w = jnp.concatenate(both_cores(gu_line), axis=0)
    down_w = jnp.zeros((hidden_slot, model), BF)
    for j, block in enumerate(both_cores(down_line)):
        down_w = lax.dynamic_update_slice_in_dim(down_w, block, (seq ^ j) * piece, 0)

    first_row = seq * tok_count
    query_pos = first_row + jnp.arange(tok_count, dtype=jnp.int32)
    seq_length = lengths[0]
    row_valid = (query_pos < seq_length).astype(jnp.float32)[:, None]
    query_valid = (query_pos < seq_length)[:, None, None]
    inputs = rows_in[0].astype(jnp.float32)
    scale_one = rms_scale(inputs)
    normed = (inputs * scale_one * gain_one.astype(jnp.float32)).astype(BF)
    normed_x = xor_blocks(normed, seq, seqs, 1)
    query_pre = xor_blocks(dot(normed_x, query_w), slot, slots, 1)
    kv_pre = dot(normed_x, kv_w)
    key_pre = kv_pre[:, :head_width]
    value_rows = kv_pre[:, head_width:].astype(BF)
    cosine_table, sine_table = rope_tables(query_pos, head_width)
    queries = rotate(
        query_pre.reshape(tok_count, head_count, head_width),
        cosine_table[:, None, :],
        sine_table[:, None, :],
    ).astype(BF)
    key_rows = rotate(key_pre, cosine_table, sine_table).astype(BF)
    shared = jnp.concatenate([key_rows, value_rows], axis=1) * row_valid.astype(BF)
    rim_list = []
    for hop_index in range(hop_count, 0, -1):
        rim_list.append(shifted(shared, "seq", hop_index))
    key_table = jnp.concatenate(rim_list + [shared], axis=0)
    key_part = key_table[:, :head_width]
    value_part = key_table[:, head_width:]
    key_pos = first_row - WINDOW + jnp.arange(key_count, dtype=jnp.int32)
    allowed = window_mask(query_pos, key_pos, seq_length)[:, None, :]
    allowed_float = allowed.astype(jnp.float32)
    flat_queries = queries.reshape(tok_count * head_count, head_width)

    def score_rows():
        raw_scores = dot(flat_queries, key_part.T)
        raw_scores = raw_scores.reshape(tok_count, head_count, key_count) * scaling
        return jnp.where(allowed, raw_scores, NEGATIVE)

    masked = score_rows()
    row_max = jnp.max(masked, axis=-1, keepdims=True)
    exponent_rows = jnp.exp(masked - row_max) * allowed_float
    row_sum = jnp.sum(exponent_rows, axis=-1, keepdims=True)
    row_denom = jnp.where(query_valid, row_sum, 1.0)
    prob_rows = (exponent_rows / row_denom).astype(BF)
    log_total = row_max + jnp.log(row_denom)
    flat_probs = prob_rows.reshape(tok_count * head_count, key_count)
    attended = dot(flat_probs, value_part)
    attended = attended.reshape(tok_count, head_count * head_width).astype(BF)
    attended_x = xor_blocks(attended, seq, seqs, 1)
    middle = inputs + xor_blocks(dot(attended_x, out_w), slot, slots, 1)
    scale_two = rms_scale(middle)
    normed_two = (middle * scale_two * gain_two.astype(jnp.float32)).astype(BF)

    normed_two_all = jnp.concatenate(
        gather_slot(xor_blocks(normed_two, seq, seqs, 1)), axis=0
    )
    down_in = rows_cot[0] * row_valid.astype(BF)
    down_in_all = jnp.concatenate(gather_slot(down_in), axis=0)
    gu_out = dot(normed_two_all, gu_w)
    gate_out = gu_out[:, :hidden_slot]
    up_out = gu_out[:, hidden_slot:]
    sig_gate = jax.nn.sigmoid(gate_out)
    hidden = (gate_out * sig_gate * up_out).astype(BF)
    down_part = dot(hidden, down_w).astype(BF)

    def token_blocks(values):
        return [values[j * tok_count : (j + 1) * tok_count] for j in range(slots)]

    result = middle + scatter_slot(token_blocks(down_part)) * row_valid

    grad_down = dot_tn(hidden, down_in_all).astype(BF)
    grad_hidden = dot_nt(down_in_all, down_w)
    grad_gate = grad_hidden * up_out * sig_gate * (1.0 + gate_out * (1.0 - sig_gate))
    grad_up = grad_hidden * gate_out * sig_gate
    grad_gu = jnp.concatenate([grad_gate.astype(BF), grad_up.astype(BF)], axis=1)
    grad_normed_two = dot_nt(grad_gu, gu_w).astype(BF)
    grad_gu_w = dot_tn(normed_two_all, grad_gu).astype(BF)
    grad_normed_two = xor_blocks(scatter_slot(token_blocks(grad_normed_two)), seq, seqs, 1)

    def row_blocks(values):
        return [values[j * rows_dev : (j + 1) * rows_dev] for j in range(seqs)]

    own_down = scatter_seq(
        [lax.dynamic_slice_in_dim(grad_down, (seq ^ j) * piece, piece, 0) for j in range(seqs)]
    ).astype(BF)
    own_gu = scatter_seq(row_blocks(grad_gu_w)).astype(BF)

    unit_two = middle * scale_two
    grad_gain_two = jnp.sum(grad_normed_two * unit_two, axis=0)
    grad_middle = rows_cot[0].astype(F32) + norm_back(
        grad_normed_two, unit_two, scale_two, gain_two
    )
    branch_grad = grad_middle.astype(BF)
    branch_x = xor_blocks(branch_grad, slot, slots, 1)

    def col_blocks(values):
        width = values.shape[1] // slots
        return [values[:, j * width : (j + 1) * width] for j in range(slots)]

    attended_all = jnp.concatenate(gather_slot(attended_x), axis=0)
    branch_all = jnp.concatenate(trade_slot(col_blocks(branch_x)), axis=0)
    own_out = scatter_seq(row_blocks(dot_tn(attended_all, branch_all).astype(BF))).astype(BF)

    grad_attended = xor_blocks(dot_nt(branch_x, out_w).astype(BF), seq, seqs, 1)
    flat_grad = grad_attended.reshape(tok_count * head_count, head_width)
    probs_float = jnp.exp(score_rows() - log_total) * allowed_float
    grad_probs = dot(flat_grad, value_part.T)
    grad_probs = grad_probs.reshape(tok_count, head_count, key_count)
    grad_scores = probs_float * (
        grad_probs - jnp.sum(probs_float * grad_probs, axis=-1, keepdims=True)
    )
    flat_scores = grad_scores.astype(BF).reshape(tok_count * head_count, key_count)
    grad_queries = dot(flat_scores, key_part) * scaling
    grad_keys = dot(flat_scores.T, flat_queries) * scaling
    grad_values = dot(flat_probs.T, flat_grad)
    grad_table = jnp.concatenate([grad_keys, grad_values], axis=1)
    own_grad = grad_table[WINDOW:] + kv_cot[0].astype(jnp.float32)
    for hop_index in range(1, hop_count + 1):
        lower = (hop_count - hop_index) * tok_count
        own_grad = own_grad + shifted(
            grad_table[lower : lower + tok_count].astype(BF), "seq", -hop_index
        ).astype(jnp.float32)
    own_grad = own_grad * row_valid
    grad_key_pre = rotate(own_grad[:, :head_width], cosine_table, -sine_table).astype(BF)
    grad_value = own_grad[:, head_width:].astype(BF)
    grad_kv_pre = jnp.concatenate([grad_key_pre, grad_value], axis=1)
    grad_query_pre = rotate(
        grad_queries.reshape(tok_count, head_count, head_width),
        cosine_table[:, None, :],
        -sine_table[:, None, :],
    )
    grad_query_pre = grad_query_pre.reshape(tok_count, head_count * head_width).astype(BF)
    grad_query_x = xor_blocks(grad_query_pre, slot, slots, 1)
    grad_normed = xor_blocks(
        dot_nt(grad_query_x, query_w) + dot_nt(grad_kv_pre, kv_w), seq, seqs, 1
    )
    unit_one = inputs * scale_one
    grad_gain_one = jnp.sum(grad_normed * unit_one, axis=0)
    grad_inputs = grad_middle + norm_back(grad_normed, unit_one, scale_one, gain_one)

    normed_all = jnp.concatenate(gather_slot(normed_x), axis=0)
    traded = trade_slot(
        [jnp.concatenate([block, grad_kv_pre], axis=1) for block in col_blocks(grad_query_x)]
    )
    grad_qkv_w = dot_tn(normed_all, jnp.concatenate(traded, axis=0)).astype(BF)
    gain_grads = jnp.stack([grad_gain_one, grad_gain_two], axis=0)
    gain_grads = xor_blocks(gain_grads, seq, seqs, 1).astype(BF)
    qkv_blocks = []
    for j, block in enumerate(row_blocks(grad_qkv_w)):
        extra = gain_grads[:, j * rows_dev : (j + 1) * rows_dev]
        extra = jnp.pad(extra, ((0, 14), (0, block.shape[1] - rows_dev)))
        qkv_blocks.append(jnp.concatenate([block, extra], axis=0))
    own_qkv = scatter_seq(qkv_blocks)
    own_query = jnp.concatenate([own_qkv[:, :cols_slot], ], axis=1).astype(BF)

    def slot_columns(blocks):
        return xor_blocks(jnp.concatenate(blocks, axis=1), slot, slots, 1).astype(F32)

    query_blocks = gather_slot(own_query)
    query_grad = slot_columns([block[:rows_dev] for block in query_blocks])
    gain_total = sum(block[rows_dev : rows_dev + 2, :rows_dev].astype(F32) for block in query_blocks)
    out_grad_w = slot_columns(gather_slot(own_out))
    down_grad = xor_blocks(
        jnp.concatenate(gather_slot(own_down), axis=0), slot, slots, 0
    ).astype(F32)
    gu_all = jnp.stack(gather_slot(own_gu), axis=0)
    gu_all = xor_blocks(gu_all, slot, slots, 0)

    def whole(part):
        cut = part.reshape(slots, rows_dev, seqs, piece).transpose(1, 2, 0, 3)
        return cut.reshape(rows_dev, hidden_all).astype(F32)

    gate_grad = whole(gu_all[:, :, :hidden_slot])
    up_grad = whole(gu_all[:, :, hidden_slot:])
    return (
        result.astype(BF)[None],
        shared[None],
        grad_inputs.astype(BF)[None],
        gain_total[0],
        query_grad,
        own_qkv[:rows_dev, cols_slot : cols_slot + head_width],
        own_qkv[:rows_dev, cols_slot + head_width : cols_slot + kv_width],
        out_grad_w,
        gain_total[1],
        gate_grad,
        up_grad,
        down_grad,
    )


def solution(mesh):
    placed = (
        P("slot", "seq", None),
        P("slot"),
        P("seq"),
        P("seq", None),
        P("seq", None),
        P("seq", None),
        P("seq", None),
        P("seq"),
        P("seq", None),
        P("seq", None),
        P("seq", None),
        P("slot", "seq", None),
        P("slot", "seq", None),
    )
    return jax.shard_map(
        shards,
        mesh=mesh,
        in_specs=placed,
        out_specs=(
            P("slot", "seq", None),
            P("slot", "seq", None),
            P("slot", "seq", None),
            P("seq"),
            P("seq", None),
            P("seq", None),
            P("seq", None),
            P("seq", None),
            P("seq"),
            P("seq", None),
            P("seq", None),
            P("seq", None),
        ),
        check_vma=False,
    )
```

```python
import functools

import jax
import jax.numpy as jnp
from jax import lax
from jax.experimental import pallas as pl
from jax.experimental.pallas import tpu as pltpu
from jax.sharding import PartitionSpec as P

WINDOW = 512


EPSILON = 1e-05
THETA = 10000.0
NEGATIVE = -1e30
BF = jnp.bfloat16
F32 = jnp.float32


def swap(block, axis, mask):
    return lax.ppermute(block, axis, [(i, i ^ mask) for i in range(lax.axis_size(axis))])


def gather_near(block):
    count = lax.axis_size("slot")
    if count != 4:
        return [block] + [swap(block, "slot", j) for j in range(1, count)]
    return [block, swap(block, "slot", 1), swap(block, "slot", 2)]


def gather_far(near):
    if lax.axis_size("slot") != 4:
        return []
    half = near[0].shape[0] // 2
    return [swap(near[1][:half], "slot", 2), swap(near[2][half:], "slot", 1)]


def scatter_pass(parts):
    if lax.axis_size("slot") != 4:
        return []
    return [swap(parts[5], "slot", 2), swap(parts[6], "slot", 1)]


def scatter_near(parts):
    if lax.axis_size("slot") != 4:
        return [swap(parts[j], "slot", j) for j in range(1, len(parts))]
    return [swap(parts[2], "slot", 1), swap(parts[3], "slot", 2)]


def scatter_far(parts, passed):
    if lax.axis_size("slot") != 4:
        return []
    low, high = passed
    return [
        swap((parts[1].astype(F32) + low.astype(F32)).astype(BF), "slot", 1),
        swap((parts[4].astype(F32) + high.astype(F32)).astype(BF), "slot", 2),
    ]


def scatter_total(parts, near, far):
    own = parts[0].astype(F32)
    if lax.axis_size("slot") != 4:
        for part in near:
            own = own + part.astype(F32)
        return own
    first = jnp.concatenate([far[0], near[0]], axis=0).astype(F32)
    second = jnp.concatenate([near[1], far[1]], axis=0).astype(F32)
    return own + first + second


def trade_slot(blocks):
    return [blocks[0]] + [swap(blocks[j], "slot", j) for j in range(1, len(blocks))]


def line_near(block):
    count = lax.axis_size("seq")
    if count != 8:
        return [block] + [swap(block, "seq", j) for j in range(2, count, 2)]
    return [block, swap(block, "seq", 2), swap(block, "seq", 6)]


def line_far(near):
    if lax.axis_size("seq") != 8:
        return []
    return [swap(near[2], "seq", 2)]


def line_all(near, far):
    return near[:2] + far + near[2:]


def shifted(block, axis, distance):
    devices = range(lax.axis_size(axis))
    route = [(i - distance, i) for i in devices if i - distance in devices]
    return lax.ppermute(block, axis, route)


def rope_tables(positions, head_width):
    half_width = head_width // 2
    exponent = jnp.arange(half_width, dtype=jnp.float32) * (2.0 / head_width)
    frequency = THETA ** (-exponent)
    angles = positions.astype(jnp.float32)[:, None] * frequency[None, :]
    return (jnp.cos(angles), jnp.sin(angles))


def dot(left, right):
    return jnp.dot(left, right, preferred_element_type=F32)


def dot_nt(left, right):
    return lax.dot_general(left, right, (((1,), (1,)), ((), ())), preferred_element_type=F32)


def dot_tn(left, right):
    return lax.dot_general(left, right, (((0,), (0,)), ((), ())), preferred_element_type=F32)


VMEM = pl.BlockSpec(memory_space=pltpu.VMEM)
SMEM = pl.BlockSpec(memory_space=pltpu.SMEM)
ANY = pl.BlockSpec(memory_space=pl.ANY)
BIG = pltpu.CompilerParams(vmem_limit_bytes=56 * 1024 * 1024)


def line_sums(mine, passed):
    count = lax.axis_size("seq") // 2
    rows = mine.shape[0] // count
    out = []
    for k in range(count):
        part = slice(k * rows, (k + 1) * rows)
        total = mine[part].astype(F32) + passed[part].astype(F32)
        out.append(total.astype(BF) if k else total)
    return out


def line_first(blocks):
    if len(blocks) != 4:
        return [swap(blocks[k], "seq", 2 * k) for k in range(1, len(blocks))]
    return [swap(blocks[1], "seq", 2), swap(blocks[2], "seq", 2)]


def line_second(blocks, first):
    if len(blocks) != 4:
        return []
    return [swap((blocks[3].astype(F32) + first[1].astype(F32)).astype(BF), "seq", 6)]


def line_total(blocks, first, second):
    parts = first[:1] + second if len(blocks) == 4 else first
    total = blocks[0]
    for part in parts:
        total = total + part.astype(F32)
    return total


def line_place(block, seq, count):
    away = block ^ seq
    return (away >> 1) + (away & 1) * (count // 2)


def line_block(place, seq, count):
    half = count // 2
    return seq ^ (2 * place if place < half else 2 * (place - half) + 1)


def line_block_at(spot, seq, count):
    half = count // 2
    return seq ^ (2 * (spot % half) + spot // half)


def line_order(values, seq, count):
    width = values.shape[1] // count
    return jnp.concatenate(
        [
            lax.dynamic_slice_in_dim(values, line_block(m, seq, count) * width, width, 1)
            for m in range(count)
        ],
        axis=1,
    )


def rms_of(values):
    return lax.rsqrt(jnp.mean(values * values, axis=-1, keepdims=True) + EPSILON)


def turn(values, cosine, sine):
    return values * cosine + pltpu.roll(values, values.shape[1] // 2, 1) * sine


def at(block, width):
    return pl.ds(pl.multiple_of(block * width, width), width)


def grouped(refs, counts):
    out, start = [], 0
    for count in counts:
        out.append(refs[start : start + count])
        start += count
    return out


def chunk_of(pieces, c, count):
    if len(pieces) == count:
        return pieces[c][...]
    rows = pieces[0].shape[0] // count
    return pieces[0][c * rows : (c + 1) * rows]


def piece_dot(left, pieces):
    total, row = None, 0
    for ref in pieces:
        rows = ref.shape[0]
        part = dot(left[:, row : row + rows], ref[...])
        total = part if total is None else total + part
        row += rows
    return total


def project_kernel(shape, *refs):
    counts, seqs = shape
    slots, count, chunks = len(counts), sum(counts), max(counts)
    place, rows_ref, gain_ref, valid_ref, cos_ref, sin_ref = refs[:6]
    mine = grouped(refs[6 : 6 + count], counts)
    theirs = grouped(refs[6 + count : 6 + 2 * count], counts)
    kv_mine, kv_theirs = refs[6 + 2 * count : 8 + 2 * count]
    normed_ref, query_ref, shared_ref, line_ref = refs[8 + 2 * count :]
    seq = place[0]
    model = rows_ref.shape[1]
    half = model // 2
    width = model // seqs
    scale = rms_of(rows_ref[...].astype(F32))
    for m in range(seqs):
        block = at(line_block(m, seq, seqs), width)
        to = slice(m * width, (m + 1) * width)
        part = rows_ref[:, block].astype(F32)
        part = (part * scale * gain_ref[:, to]).astype(BF)
        normed_ref[:, block] = part
        line_ref[:, to] = part
    cosine, sine = cos_ref[...], sin_ref[...]
    head = cosine.shape[1]
    left, right = line_ref[:, :half], line_ref[:, half:]
    col = 0
    for i in range(slots):
        total = piece_dot(left, mine[i]) + piece_dot(right, theirs[i])
        for h in range(total.shape[1] // head):
            turned = turn(total[:, h * head : (h + 1) * head], cosine, sine)
            query_ref[:, col : col + head] = turned.astype(BF)
            col += head
    kv = dot(left, kv_mine[...]) + dot(right, kv_theirs[...])
    valid = valid_ref[...]
    shared_ref[:, :head] = (turn(kv[:, :head], cosine, sine) * valid).astype(BF)
    shared_ref[:, head:] = (kv[:, head:] * valid).astype(BF)


def set_bias(place, bias_ref, step):
    @pl.when(step == 0)
    def _():
        toks, keys = bias_ref.shape
        first = place[0] * toks
        query = first + lax.broadcasted_iota(jnp.int32, (toks, keys), 0)
        key = first - WINDOW + lax.broadcasted_iota(jnp.int32, (toks, keys), 1)
        length = place[2]
        away = query - key
        good = (key >= 0) & (key < length) & (away >= 0) & (away < WINDOW) & (query < length)
        bias_ref[...] = jnp.where(good, 0.0, NEGATIVE)


def softmax_rows(place, query, keys, bias):
    head = query.shape[1]
    scores = dot_nt(query, keys) * (head**-0.5) + bias
    grown = jnp.exp(scores - jnp.max(scores, axis=-1, keepdims=True))
    toks = query.shape[0]
    pos = place[0] * toks + lax.broadcasted_iota(jnp.int32, (toks, 1), 0)
    total = jnp.sum(grown, axis=-1, keepdims=True)
    return grown * jnp.where(pos < place[2], 1.0 / total, 0.0)


def attend_kernel(rims, late, place, query_ref, *refs):
    table = refs[: rims + 1]
    out_ref, bias_ref = refs[rims + 1 + late :]
    set_bias(place, bias_ref, pl.program_id(0))
    head = query_ref.shape[1]
    keys = jnp.concatenate([ref[:, :head] for ref in table], axis=0)
    values = jnp.concatenate([ref[:, head:] for ref in table], axis=0)
    probs = softmax_rows(place, query_ref[...], keys, bias_ref[...])
    out_ref[...] = dot(probs.astype(BF), values).astype(BF)


def attend_back_kernel(rims, late, place, query_ref, grad_ref, *refs):
    table = refs[: rims + 1]
    cos_ref, sin_ref = refs[rims + 1 : rims + 3]
    gq_ref, gkv_ref, bias_ref = refs[rims + 3 + late :]
    step = pl.program_id(0)
    set_bias(place, bias_ref, step)

    @pl.when(step == 0)
    def _():
        gkv_ref[...] = jnp.zeros_like(gkv_ref)

    head = query_ref.shape[1]
    scaling = head**-0.5
    keys = jnp.concatenate([ref[:, :head] for ref in table], axis=0)
    values = jnp.concatenate([ref[:, head:] for ref in table], axis=0)
    query, grad = query_ref[...], grad_ref[...]
    probs = softmax_rows(place, query, keys, bias_ref[...])
    grad_probs = dot_nt(grad, values)
    both = probs * grad_probs
    grad_scores = (both - probs * jnp.sum(both, axis=-1, keepdims=True)).astype(BF)
    grad_query = dot(grad_scores, keys) * scaling
    gq_ref[...] = turn(grad_query, cos_ref[...], -sin_ref[...]).astype(BF)
    gkv_ref[:, :head] += dot_tn(grad_scores, query) * scaling
    gkv_ref[:, head:] += dot_tn(probs.astype(BF), grad)


def out_kernel(shape, *refs):
    counts, seqs = shape
    slots, count, chunks = len(counts), sum(counts), max(counts)
    place, att_ref, rows_ref, gain_ref = refs[:4]
    mine = grouped(refs[4 : 4 + count], counts)
    theirs = grouped(refs[4 + count : 4 + 2 * count], counts)
    middle_ref, normed_ref, plain_ref = refs[4 + 2 * count :]
    seq, slot = place[0], place[1]
    model = rows_ref.shape[1]
    half = model // 2
    width = model // seqs
    left, right = att_ref[:, :half], att_ref[:, half:]
    for i in range(slots):
        total = piece_dot(left, mine[i]) + piece_dot(right, theirs[i])
        to = at(slot ^ i, total.shape[1])
        middle_ref[:, to] = rows_ref[:, to].astype(F32) + total
    scale = rms_of(middle_ref[...])
    for m in range(seqs):
        to = at(line_block(m, seq, seqs), width)
        gain = gain_ref[:, m * width : (m + 1) * width]
        normed_ref[:, to] = (middle_ref[:, to] * scale * gain).astype(BF)
        plain_ref[:, to] = att_ref[:, m * width : (m + 1) * width]


def mid_back_kernel(shape, *refs):
    counts, seqs = shape
    slots, count, chunks = len(counts), sum(counts), max(counts)
    place, grad_ref, middle_ref, cot_ref, gain_ref = refs[:5]
    mine = grouped(refs[5 : 5 + count], counts)
    theirs = grouped(refs[5 + count : 5 + 2 * count], counts)
    gmid_ref, gatt_ref, ggain_ref = refs[5 + 2 * count : 8 + 2 * count]
    branch = refs[8 + 2 * count :]
    seq, slot = place[0], place[1]
    model = middle_ref.shape[1]
    half = model // 2
    width = model // seqs
    scale = rms_of(middle_ref[...])
    mean = 0.0
    for m in range(seqs):
        to = at(line_block(m, seq, seqs), width)
        here = slice(m * width, (m + 1) * width)
        grad = grad_ref[:, to]
        unit = middle_ref[:, to] * scale
        ggain_ref[:, to] = jnp.sum(grad * unit, axis=0, keepdims=True)
        scaled = grad * gain_ref[:, here]
        gmid_ref[:, to] = scaled
        mean = mean + jnp.sum(scaled * unit, axis=1, keepdims=True)
    mean = mean * (1.0 / model)
    gmid_ref[...] = cot_ref[...].astype(F32) + scale * (
        gmid_ref[...] - middle_ref[...] * (scale * mean)
    )
    out_cols = model // slots
    for i in range(slots):
        branch[i][...] = gmid_ref[:, at(slot ^ i, out_cols)].astype(BF)
    for pieces, start in ((mine, 0), (theirs, half)):
        row = start
        for c in range(chunks):
            rows = half // chunks
            total = dot_nt(branch[0][...], chunk_of(pieces[0], c, chunks))
            for i in range(1, slots):
                total = total + dot_nt(branch[i][...], chunk_of(pieces[i], c, chunks))
            gatt_ref[:, row : row + rows] = total.astype(BF)
            row += rows


def input_back_kernel(shape, *refs):
    counts, seqs = shape
    slots, count, chunks = len(counts), sum(counts), max(counts)
    place, gq_ref, gkv_ref, rows_ref, gmid_ref, gain_ref = refs[:6]
    mine = grouped(refs[6 : 6 + count], counts)
    theirs = grouped(refs[6 + count : 6 + 2 * count], counts)
    kv_mine, kv_theirs = refs[6 + 2 * count : 8 + 2 * count]
    out_ref, ggain_ref, scaled_ref = refs[8 + 2 * count :]
    seq = place[0]
    model = rows_ref.shape[1]
    half = model // 2
    width = model // seqs
    cols = model // slots
    rows_in = rows_ref[...].astype(F32)
    scale = rms_of(rows_in)
    mean = 0.0
    for pieces, kv_ref, start in ((mine, kv_mine, 0), (theirs, kv_theirs, half)):
        row = 0
        for c in range(chunks):
            rows = half // chunks
            total = dot_nt(gkv_ref[...], kv_ref[row : row + rows])
            for i in range(slots):
                total = total + dot_nt(
                    gq_ref[:, i * cols : (i + 1) * cols], chunk_of(pieces[i], c, chunks)
                )
            for b in range(rows // width):
                m = (start + row) // width + b
                here = slice(m * width, (m + 1) * width)
                to = at(line_block(m, seq, seqs), width)
                grad = total[:, b * width : (b + 1) * width]
                unit = rows_ref[:, to].astype(F32) * scale
                ggain_ref[:, to] = jnp.sum(grad * unit, axis=0, keepdims=True)
                scaled = grad * gain_ref[:, here]
                scaled_ref[:, to] = scaled
                mean = mean + jnp.sum(scaled * unit, axis=1, keepdims=True)
            row += rows
    mean = mean * (1.0 / model)
    out_ref[...] = (
        gmid_ref[...] + scale * (scaled_ref[...] - rows_in * (scale * mean))
    ).astype(BF)


def share_kernel(slots, seqs, place, gate_ref, up_ref, out_ref):
    piece = gate_ref.shape[1] // (slots * seqs)
    width = piece * seqs
    for s in range(slots):

        @pl.when(place[1] == s)
        def _():
            for n, ref in enumerate((gate_ref, up_ref)):
                parts = [
                    ref[:, (q * slots + s) * piece : (q * slots + s + 1) * piece]
                    for q in range(seqs)
                ]
                out_ref[:, n * width : (n + 1) * width] = jnp.concatenate(parts, axis=1)


def parts_product(left, right):
    total, block, row = None, 0, 0
    for ref in left:
        rows = ref.shape[0]
        part = dot_tn(ref[...], right[block][row : row + rows])
        total = part if total is None else total + part
        row += rows
        if row == right[block].shape[0]:
            block, row = block + 1, 0
    return total


def line_grads_kernel(count, slots, place, *refs):
    normed, attended = refs[:count], refs[count : 2 * count]
    traded, branch = refs[2 * count : 2 * count + slots], refs[2 * count + slots :][:slots]
    gain_ref, out_ref = refs[2 * count + 2 * slots], refs[-1]
    first = parts_product(normed, traded)
    second = parts_product(attended, branch)
    start = first.shape[1]
    end = start + second.shape[1]
    out_ref[:, :start] = first.astype(BF)
    out_ref[:, start:end] = second.astype(BF)
    out_ref[:, end:] = gain_ref[...]


def cut_store(total, outs):
    row = 0
    for ref in outs:
        rows = ref.shape[0]
        ref[...] = total[row : row + rows].astype(BF)
        row += rows


def gate_kernel(count, *refs):
    tokens = refs[:count]
    wgate_ref, wup_ref, all_ref, gate_ref, up_ref, hidden_ref = refs[count:]

    @pl.when(pl.program_id(0) == 0)
    def _():
        row = 0
        for ref in tokens:
            all_ref[row : row + ref.shape[0]] = ref[...]
            row += ref.shape[0]

    tile = wgate_ref.shape[1]
    both = dot(all_ref[...], jnp.concatenate([wgate_ref[...], wup_ref[...]], axis=1))
    gate, up = both[:, :tile], both[:, tile:]
    gate_ref[...] = gate.astype(BF)
    up_ref[...] = up.astype(BF)
    hidden_ref[...] = (gate * jax.nn.sigmoid(gate) * up).astype(BF)


def rows_kernel(transposed, late, left_ref, right_ref, *refs):
    right = right_ref[...]
    total = dot_nt(left_ref[...], right) if transposed else dot(left_ref[...], right)
    cut_store(total, refs[late:])


def unline_kernel(seqs, place, *refs):
    out_ref = refs[seqs]
    for m in range(seqs):
        rows = refs[m].shape[0]
        to = pl.ds(pl.multiple_of(line_block(m, place[0], seqs) * rows, rows), rows)
        out_ref[to] = refs[m][...]


def unshare_kernel(slots, seqs, place, part_ref, out_ref):
    piece = part_ref.shape[2] // seqs
    parts = []
    for q in range(seqs):
        for s in range(slots):
            part = part_ref[s, :, q * piece : (q + 1) * piece]
            parts.append(part.astype(F32))
    out_ref[...] = jnp.concatenate(parts, axis=1)


def tie(value, *after):
    return pl.pallas_call(
        lambda *refs: None,
        out_shape=jax.ShapeDtypeStruct(value.shape, value.dtype),
        in_specs=[ANY] * (1 + len(after)),
        out_specs=ANY,
        input_output_aliases={0: 0},
    )(value, *after)


def fence(values, after):
    count = len(values)
    return list(
        pl.pallas_call(
            lambda *refs: None,
            out_shape=[jax.ShapeDtypeStruct(value.shape, value.dtype) for value in values],
            in_specs=[ANY] * (count + len(after)),
            out_specs=[ANY] * count,
            input_output_aliases={k: k for k in range(count)},
        )(*values, *after)
    )


class Flow:
    def __init__(self):
        self.now = []

    def at(self, *values):
        self.now = list(values)

    def go(self, *values):
        kept = {id(value) for value in values}
        return fence(list(values), [value for value in self.now if id(value) not in kept])


def call(kernel, inputs, late, out_shape, in_specs=None, scratch=()):
    count = len(inputs)
    single = not isinstance(out_shape, (tuple, list))

    def run(*refs):
        kernel(*refs[:count], *refs[count + len(late) :])

    return pl.pallas_call(
        run,
        out_shape=out_shape,
        in_specs=[SMEM] + [VMEM] * (count - 1) + [ANY] * len(late),
        out_specs=VMEM if single else (VMEM,) * len(out_shape),
        scratch_shapes=list(scratch),
        compiler_params=BIG,
    )(*inputs, *late)


def shape_of(rows, cols, kind):
    return jax.ShapeDtypeStruct((rows, cols), kind)


def shards(
    rows_in,
    lengths,
    norm1_gain,
    w_query,
    w_key,
    w_value,
    w_out,
    norm2_gain,
    w_gate,
    w_up,
    w_down,
    rows_cot,
    kv_cot,
):
    slots = lax.axis_size("slot")
    seqs = lax.axis_size("seq")
    slot = lax.axis_index("slot")
    seq = lax.axis_index("seq")
    tok_count = rows_in.shape[1]
    model = rows_in.shape[2]
    head_width = w_key.shape[1]
    head_count = w_query.shape[1] // head_width
    hop_count = WINDOW // tok_count
    key_count = WINDOW + tok_count
    rows_dev = w_query.shape[0]
    cols_slot = w_query.shape[1] // slots
    out_slot = w_out.shape[1] // slots
    hidden_all = w_gate.shape[1]
    piece = hidden_all // (slots * seqs)
    hidden_slot = piece * seqs
    half = model // 2
    extra = 16
    place = jnp.stack([seq, slot, lengths[0]]).astype(jnp.int32)
    rows_own, cot_own = rows_in[0], rows_cot[0]

    first_row = seq * tok_count
    query_pos = first_row + jnp.arange(tok_count, dtype=jnp.int32)
    row_valid = (query_pos < lengths[0]).astype(F32)[:, None]
    flow = Flow()

    gains = jnp.stack([norm1_gain, norm2_gain], axis=0)
    pack = jnp.concatenate(
        [lax.dynamic_slice_in_dim(w_query, slot * cols_slot, cols_slot, 1), w_key, w_value], axis=1
    )
    gains = jnp.pad(gains, ((0, extra - 2), (cols_slot, pack.shape[1] - cols_slot - rows_dev)))
    pack = jnp.concatenate([pack, gains], axis=0)
    pack_near = line_near(pack)
    cot_near = gather_near(cot_own * row_valid.astype(BF))
    gu_share = call(
        functools.partial(share_kernel, slots, seqs),
        (place, w_gate, w_up),
        (),
        shape_of(rows_dev, 2 * hidden_slot, BF),
    )
    out_share = lax.dynamic_slice_in_dim(w_out, slot * out_slot, out_slot, 1)
    down_share = lax.dynamic_slice_in_dim(w_down, slot * piece, piece, 0)
    flow.at(*pack_near[1:], *cot_near[1:], gu_share)

    *pack_near[1:], out_share = flow.go(*pack_near[1:], out_share)
    *cot_near[1:], down_share = flow.go(*cot_near[1:], down_share)
    pack_far = line_far(pack_near)
    out_near = line_near(out_share)
    cot_far = gather_far(cot_near)
    flow.at(*pack_far, *out_near[1:], *cot_far)

    pack_line = line_all(pack_near, pack_far)
    query_line = jnp.concatenate([block[:rows_dev, :cols_slot] for block in pack_line], axis=0)
    kv_gain = jnp.concatenate([block[:, cols_slot:] for block in pack_line], axis=0)
    query_line, kv_gain, out_near[-1], gu_share = flow.go(
        query_line, kv_gain, out_near[-1], gu_share
    )
    gu_w = lax.all_gather(gu_share, "seq", axis=0, tiled=True)
    down_w = lax.all_gather(down_share, "seq", axis=0, tiled=True)
    query_near = gather_near(query_line)
    query_other = [swap(query_line, "seq", 1)]
    kv_other = swap(kv_gain, "seq", 1)
    out_far = line_far(out_near)
    flow.at(*query_near[1:], query_other[0], kv_other, *out_far)

    query_near[1:] = flow.go(*query_near[1:])
    query_far = gather_far(query_near)
    query_other += [swap(part, "seq", 1) for part in query_near[1:]]
    flow.at(*query_far, *query_other[1:])

    *query_far, out_line = flow.go(
        *query_far, jnp.concatenate(line_all(out_near, out_far), axis=0)
    )
    query_other += [swap(part, "seq", 1) for part in query_far]
    query_w = query_near + query_far + query_other
    out_near = gather_near(out_line)
    flow.at(*query_w[len(query_near) :])
    kv_w, gain_line = [], []
    for part in (kv_gain, kv_other):
        part = part.reshape(seqs // 2, rows_dev + extra, -1)
        kv_w.append(part[:, :rows_dev].reshape(half, -1))
        gain_line.append(part[:, rows_dev : rows_dev + 2, :rows_dev])
    gain_line = jnp.concatenate(gain_line, axis=0).transpose(1, 0, 2).reshape(2, 1, model)
    gain_line = gain_line.astype(F32)
    gain_one, gain_two = gain_line[0], gain_line[1]
    shape = ((1, 1, 1, 2) if slots == 4 else (1,) * slots, seqs)

    cosine, sine = rope_tables(query_pos, head_width)
    cosine = jnp.concatenate([cosine, cosine], axis=1)
    sine = jnp.concatenate([-sine, sine], axis=1)
    normed, queries, shared = call(
        functools.partial(project_kernel, shape),
        (place, rows_own, gain_one, row_valid, cosine, sine, *query_w, *kv_w),
        (),
        (
            shape_of(tok_count, model, BF),
            shape_of(tok_count, head_count * head_width, BF),
            shape_of(tok_count, 2 * head_width, BF),
        ),
        scratch=[pltpu.VMEM((tok_count, model), BF)],
    )
    out_other = [swap(out_near[0], "seq", 1)]
    table = [shifted(shared, "seq", hop) for hop in range(hop_count, 0, -1)] + [shared]
    flow.at(*table[:-1], out_other[0], *out_near[1:])

    slot_heads = head_count // slots
    block_heads = rows_dev // head_width

    def own_col(p, place):
        return (0, p)

    def line_col(p, place):
        head = (place[1] ^ (p // slot_heads)) * slot_heads + p % slot_heads
        spot = line_place(head // block_heads, place[0], seqs)
        return (0, spot * block_heads + head % block_heads)

    def fixed(p, place):
        return (0, 0)

    head_own = pl.BlockSpec((tok_count, head_width), own_col)
    head_line = pl.BlockSpec((tok_count, head_width), line_col)
    table_spec = [pl.BlockSpec((tok_count, 2 * head_width), fixed)] * (hop_count + 1)
    angle_spec = [pl.BlockSpec((tok_count, head_width), fixed)] * 2
    bias_scratch = [pltpu.VMEM((tok_count, key_count), F32)]
    out_near[1:] = flow.go(*out_near[1:])
    out_far = gather_far(out_near)
    out_other += [swap(part, "seq", 1) for part in out_near[1:]]
    late = out_near[1:]
    attended = pl.pallas_call(
        functools.partial(attend_kernel, hop_count, len(late)),
        out_shape=shape_of(tok_count, head_count * head_width, BF),
        grid_spec=pltpu.PrefetchScalarGridSpec(
            num_scalar_prefetch=1,
            grid=(head_count,),
            in_specs=[head_own] + table_spec + [ANY] * len(late),
            out_specs=head_line,
            scratch_shapes=bias_scratch,
        ),
        compiler_params=BIG,
    )(place, queries, *table, *late)
    flow.at(*out_far, *out_other[1:], attended)
    if out_far:
        out_far = flow.go(*out_far)
    out_other += [swap(part, "seq", 1) for part in out_far]
    out_w = out_near + out_far + out_other
    middle, normed_two, attended = call(
        functools.partial(out_kernel, shape),
        (place, attended, rows_own, gain_two, *out_w),
        (),
        (
            shape_of(tok_count, model, F32),
            shape_of(tok_count, model, BF),
            shape_of(tok_count, model, BF),
        ),
    )

    normed_two_near = gather_near(normed_two)
    cot_rows = jnp.concatenate(cot_near + cot_far, axis=0)
    flow.at(*normed_two_near[1:], cot_rows)
    normed_two_near[1:] = flow.go(*normed_two_near[1:])
    normed_two_parts = normed_two_near + gather_far(normed_two_near)
    flow.at(*normed_two_parts[len(normed_two_near) - 1 :])

    normed_near = gather_near(tie(normed, *normed_two_parts[slots - 1 :]))
    tokens = slots * tok_count
    tile = 128
    if hidden_slot % tile == 0:
        steps = hidden_slot // tile
        part_spec = pl.BlockSpec((tokens, tile), lambda j: (0, j))
        normed_two_all, gate_out, up_out, hidden = pl.pallas_call(
            functools.partial(gate_kernel, len(normed_two_parts)),
            out_shape=(shape_of(tokens, model, BF),) + (shape_of(tokens, hidden_slot, BF),) * 3,
            grid=(steps,),
            in_specs=[pl.BlockSpec(part.shape, lambda j: (0, 0)) for part in normed_two_parts]
            + [
                pl.BlockSpec((model, tile), lambda j: (0, j)),
                pl.BlockSpec((model, tile), lambda j: (0, steps + j)),
            ],
            out_specs=(pl.BlockSpec((tokens, model), lambda j: (0, 0)),) + (part_spec,) * 3,
            compiler_params=BIG,
        )(*normed_two_parts, gu_w, gu_w)
        gate_out, up_out = gate_out.astype(F32), up_out.astype(F32)
    else:
        normed_two_all = jnp.concatenate(normed_two_parts, axis=0)
        gu_out = dot(normed_two_all, gu_w)
        gate_out, up_out = gu_out[:, :hidden_slot], gu_out[:, hidden_slot:]
        hidden = (gate_out * jax.nn.sigmoid(gate_out) * up_out).astype(BF)
    sig_gate = jax.nn.sigmoid(gate_out)
    cot_rows = tie(cot_rows, *normed_near[1:], hidden)
    grad_down = dot_tn(hidden, cot_rows).astype(BF)
    own_down = lax.psum_scatter(grad_down, "seq", scatter_dimension=0, tiled=True)
    *normed_near[1:], attended = fence([*normed_near[1:], attended], [cot_rows])
    normed_all = normed_near + gather_far(normed_near)
    attended_near = gather_near(attended)

    grad_hidden = dot_nt(cot_rows, down_w)
    grad_gate = grad_hidden * up_out * sig_gate * (1.0 + gate_out * (1.0 - sig_gate))
    grad_up = grad_hidden * gate_out * sig_gate
    grad_gu = jnp.concatenate([grad_gate.astype(BF), grad_up.astype(BF)], axis=1)
    grad_gu = tie(grad_gu, *normed_all[slots - 1 :], *attended_near[1:])
    half_tok = tok_count // 2
    cut_rows = [tok_count] + [half_tok] * 6 if slots == 4 else [tok_count] * slots

    def cut_product(left, right, transposed, late):
        width = 256
        depth = left.shape[1]
        right_spec = (
            pl.BlockSpec((width, depth), lambda j: (j, 0))
            if transposed
            else pl.BlockSpec((depth, width), lambda j: (0, j))
        )
        return list(
            pl.pallas_call(
                functools.partial(rows_kernel, transposed, len(late)),
                out_shape=[shape_of(rows, model, BF) for rows in cut_rows],
                grid=(model // width,),
                in_specs=[pl.BlockSpec(left.shape, lambda j: (0, 0)), right_spec]
                + [ANY] * len(late),
                out_specs=[pl.BlockSpec((rows, width), lambda j: (0, j)) for rows in cut_rows],
                compiler_params=BIG,
            )(left, right, *late)
        )

    attended_near[1:] = fence(attended_near[1:], [grad_gu])
    attended_all = attended_near + gather_far(attended_near)
    grad_parts = cut_product(grad_gu, gu_w, True, ())
    if slots == 4:
        grad_parts[5:] = fence(
            grad_parts[5:], attended_all[slots - 1 :]
        )
    passed = scatter_pass(grad_parts)
    down_parts = cut_product(tie(hidden, grad_parts[0]), down_w, False, ())
    if slots == 4:
        *passed, grad_parts[2], grad_parts[3], grad_gu = fence(
            [*passed, grad_parts[2], grad_parts[3], grad_gu], [down_parts[0]]
        )
    near = scatter_near(grad_parts)
    far = scatter_far(grad_parts, passed)
    grad_gate_w = dot_tn(normed_two_all, grad_gu[:, :hidden_slot]).astype(BF)
    grad_normed_two = scatter_total(grad_parts, near, far)
    grad_gate_w, own_down, down_parts[-1] = fence(
        [grad_gate_w, own_down, down_parts[-1]], [grad_normed_two]
    )
    own_gate = lax.psum_scatter(grad_gate_w, "seq", scatter_dimension=0, tiled=True)
    down_passed = scatter_pass(
        [*down_parts[:-2], tie(down_parts[-2], down_parts[-1]), down_parts[-1]]
    )

    grad_middle, grad_attended, grad_gain_two, *branch = call(
        functools.partial(mid_back_kernel, shape),
        (place, grad_normed_two, middle, cot_own, gain_two, *out_w),
        (grad_gate_w,),
        (
            shape_of(tok_count, model, F32),
            shape_of(tok_count, head_count * head_width, BF),
            shape_of(1, model, F32),
        )
        + (shape_of(tok_count, out_slot, BF),) * slots,
    )
    branch_all = trade_slot(branch)

    grad_query, grad_table = pl.pallas_call(
        functools.partial(attend_back_kernel, hop_count, 0),
        out_shape=(
            shape_of(tok_count, head_count * head_width, BF),
            shape_of(key_count, 2 * head_width, F32),
        ),
        grid_spec=pltpu.PrefetchScalarGridSpec(
            num_scalar_prefetch=1,
            grid=(head_count,),
            in_specs=[head_own, head_line] + table_spec + angle_spec,
            out_specs=(head_own, pl.BlockSpec((key_count, 2 * head_width), fixed)),
            scratch_shapes=bias_scratch,
        ),
        compiler_params=BIG,
    )(place, queries, grad_attended, *table, cosine, sine)
    grad_table, down_parts[2], down_parts[3], *down_passed = fence(
        [grad_table, down_parts[2], down_parts[3], *down_passed],
        branch_all[1:],
    )
    down_near = scatter_near(down_parts)
    grad_up_w = dot_tn(normed_two_all, tie(grad_gu, grad_table)[:, hidden_slot:]).astype(BF)
    own_grad = grad_table[WINDOW:] + kv_cot[0].astype(F32)
    for hop in range(1, hop_count + 1):
        lower = (hop_count - hop) * tok_count
        own_grad = own_grad + shifted(
            grad_table[lower : lower + tok_count].astype(BF), "seq", -hop
        ).astype(F32)
    own_grad = own_grad * row_valid
    grad_key = own_grad[:, :head_width]
    grad_key = grad_key * cosine - jnp.roll(grad_key, head_width // 2, axis=1) * sine
    grad_kv = jnp.concatenate([grad_key, own_grad[:, head_width:]], axis=1).astype(BF)
    grad_kv, own_down = fence([grad_kv, own_down], [grad_up_w])

    traded = [
        jnp.concatenate([grad_query[:, j * cols_slot : (j + 1) * cols_slot], grad_kv], axis=1)
        for j in range(slots)
    ]
    late = traded
    traded = trade_slot(traded)
    grad_inputs, grad_gain_one = call(
        functools.partial(input_back_kernel, shape),
        (place, grad_query, grad_kv, rows_own, grad_middle, gain_one, *query_w, *kv_w),
        late,
        (shape_of(tok_count, model, BF), shape_of(1, model, F32)),
        scratch=[pltpu.VMEM((tok_count, model), F32)],
    )
    gain_grads = jnp.concatenate([grad_gain_one, grad_gain_two], axis=0).astype(BF)
    gain_grads = jnp.pad(gain_grads.T, ((0, 0), (0, head_width - 2)))
    gain_grads, down_parts[1], own_down = fence(
        [gain_grads, down_parts[1], own_down], [grad_inputs, *traded[1:], *down_near]
    )
    own_down_near = gather_near(own_down)
    width_all = traded[0].shape[1] + branch_all[0].shape[1] + head_width
    places = seqs // 2

    def line_grads(start, late):
        def columns(m, place):
            return (0, line_block_at(start + m, place[0], seqs))

        def rows(m, place):
            return (line_block_at(start + m, place[0], seqs), 0)

        return pl.pallas_call(
            functools.partial(line_grads_kernel, len(normed_all), slots),
            out_shape=shape_of(half, width_all, BF),
            grid_spec=pltpu.PrefetchScalarGridSpec(
                num_scalar_prefetch=1,
                grid=(places,),
                in_specs=[
                    pl.BlockSpec((part.shape[0], rows_dev), columns)
                    for part in normed_all + attended_all
                ]
                + [pl.BlockSpec(part.shape, fixed) for part in traded + branch_all]
                + [pl.BlockSpec((rows_dev, head_width), rows)]
                + [ANY] * len(late),
                out_specs=pl.BlockSpec((rows_dev, width_all), lambda m, place: (m, 0)),
            ),
            compiler_params=BIG,
        )(place, *normed_all, *attended_all, *traded, *branch_all, gain_grads, *late)

    theirs = line_grads(places, ())
    down_far = scatter_far(down_parts, down_passed)
    passed = swap(theirs, "seq", 1)
    mine = line_grads(0, (theirs,))
    grad_up_w = tie(grad_up_w, own_gate, grad_inputs)
    own_up = lax.psum_scatter(grad_up_w, "seq", scatter_dimension=0, tiled=True)
    passed = tie(passed, mine)
    own_down_near[1:] = fence(own_down_near[1:], [passed])
    own_down_all = own_down_near + gather_far(own_down_near)
    line = line_sums(mine, passed)
    first = line_first(line)
    down_total = scatter_total(down_parts, down_near, down_far)
    result = (middle + down_total * row_valid).astype(BF)
    second = line_second(line, first)
    own_gate = tie(own_gate.astype(BF), own_up, result)
    gate_all = lax.all_gather(own_gate, "slot", axis=0)
    up_all = lax.all_gather(own_up.astype(BF), "slot", axis=0)
    own = line_total(line, first, second)
    kv_end = cols_slot + 2 * head_width
    shared_out = jnp.concatenate([own[:, :cols_slot], own[:, kv_end:]], axis=1).astype(BF)
    shared_near = gather_near(shared_out)
    all_own = jnp.concatenate(shared_near + gather_far(shared_near), axis=0)
    all_own = all_own.reshape(slots, rows_dev, -1)
    all_own = jnp.stack(
        [lax.dynamic_index_in_dim(all_own, slot ^ j, 0, keepdims=False) for j in range(slots)]
    )

    def by_slot(parts):
        parts = jnp.concatenate(parts, axis=0).reshape(slots, -1, parts[0].shape[1])
        return jnp.stack(
            [lax.dynamic_index_in_dim(parts, slot ^ j, 0, keepdims=False) for j in range(slots)]
        )

    def slot_columns(parts):
        return parts.transpose(1, 0, 2).reshape(rows_dev, -1).astype(F32)

    query_grad = slot_columns(all_own[:, :, :cols_slot])
    out_grad_w = slot_columns(all_own[:, :, cols_slot : cols_slot + out_slot])
    gain_total = jnp.sum(all_own[:, :, cols_slot + out_slot :][:, :, :2].astype(F32), axis=0)
    down_grad = by_slot(own_down_all).reshape(slots * piece, model).astype(F32)
    row_tile = 32

    def whole_rows(parts):
        return pl.pallas_call(
            functools.partial(unshare_kernel, slots, seqs),
            out_shape=shape_of(rows_dev, hidden_all, F32),
            grid_spec=pltpu.PrefetchScalarGridSpec(
                num_scalar_prefetch=1,
                grid=(rows_dev // row_tile,),
                in_specs=[
                    pl.BlockSpec((slots, row_tile, hidden_slot), lambda r, place: (0, r, 0))
                ],
                out_specs=pl.BlockSpec((row_tile, hidden_all), lambda r, place: (r, 0)),
            ),
            compiler_params=BIG,
        )(place, parts)

    gate_grad = whole_rows(gate_all)
    up_grad = whole_rows(up_all)
    return (
        result[None],
        shared[None],
        grad_inputs[None],
        gain_total[:, 0],
        query_grad,
        own[:, cols_slot : cols_slot + head_width].astype(F32),
        own[:, cols_slot + head_width : kv_end].astype(F32),
        out_grad_w,
        gain_total[:, 1],
        gate_grad,
        up_grad,
        down_grad,
    )


def solution(mesh):
    placed = (
        P("slot", "seq", None),
        P("slot"),
        P("seq"),
        P("seq", None),
        P("seq", None),
        P("seq", None),
        P("seq", None),
        P("seq"),
        P("seq", None),
        P("seq", None),
        P("seq", None),
        P("slot", "seq", None),
        P("slot", "seq", None),
    )
    return jax.shard_map(
        shards,
        mesh=mesh,
        in_specs=placed,
        out_specs=(
            P("slot", "seq", None),
            P("slot", "seq", None),
            P("slot", "seq", None),
            P("seq"),
            P("seq", None),
            P("seq", None),
            P("seq", None),
            P("seq", None),
            P("seq"),
            P("seq", None),
            P("seq", None),
            P("seq", None),
        ),
        check_vma=False,
    )
```

```python
import functools

import jax
import jax.numpy as jnp
from jax import lax
from jax.experimental import pallas as pl
from jax.experimental.pallas import tpu as pltpu
from jax.sharding import PartitionSpec as P

WINDOW = 512


EPSILON = 1e-05
THETA = 10000.0
NEGATIVE = -1e30
BF = jnp.bfloat16
F32 = jnp.float32


def swap(block, axis, mask):
    return lax.ppermute(block, axis, [(i, i ^ mask) for i in range(lax.axis_size(axis))])


def gather_near(block):
    count = lax.axis_size("slot")
    if count != 4:
        return [block] + [swap(block, "slot", j) for j in range(1, count)]
    return [block, swap(block, "slot", 1), swap(block, "slot", 2)]


def gather_far(near):
    if lax.axis_size("slot") != 4:
        return []
    half = near[0].shape[0] // 2
    return [swap(near[1][:half], "slot", 2), swap(near[2][half:], "slot", 1)]


def scatter_pass(parts):
    if lax.axis_size("slot") != 4:
        return []
    return [swap(parts[5], "slot", 2), swap(parts[6], "slot", 1)]


def scatter_near(parts):
    if lax.axis_size("slot") != 4:
        return [swap(parts[j], "slot", j) for j in range(1, len(parts))]
    return [swap(parts[2], "slot", 1), swap(parts[3], "slot", 2)]


def scatter_far(parts, passed):
    if lax.axis_size("slot") != 4:
        return []
    low, high = passed
    return [
        swap((parts[1].astype(F32) + low.astype(F32)).astype(BF), "slot", 1),
        swap((parts[4].astype(F32) + high.astype(F32)).astype(BF), "slot", 2),
    ]


def scatter_total(parts, near, far):
    own = parts[0].astype(F32)
    if lax.axis_size("slot") != 4:
        for part in near:
            own = own + part.astype(F32)
        return own
    first = jnp.concatenate([far[0], near[0]], axis=0).astype(F32)
    second = jnp.concatenate([near[1], far[1]], axis=0).astype(F32)
    return own + first + second


def trade_slot(blocks):
    return [blocks[0]] + [swap(blocks[j], "slot", j) for j in range(1, len(blocks))]


def line_near(block):
    count = lax.axis_size("seq")
    if count != 8:
        return [block] + [swap(block, "seq", j) for j in range(2, count, 2)]
    return [block, swap(block, "seq", 2), swap(block, "seq", 6)]


def line_far(near):
    if lax.axis_size("seq") != 8:
        return []
    return [swap(near[2], "seq", 2)]


def line_all(near, far):
    return near[:2] + far + near[2:]


def shifted(block, axis, distance):
    devices = range(lax.axis_size(axis))
    route = [(i - distance, i) for i in devices if i - distance in devices]
    return lax.ppermute(block, axis, route)


def rope_tables(positions, head_width):
    half_width = head_width // 2
    exponent = jnp.arange(half_width, dtype=jnp.float32) * (2.0 / head_width)
    frequency = THETA ** (-exponent)
    angles = positions.astype(jnp.float32)[:, None] * frequency[None, :]
    return (jnp.cos(angles), jnp.sin(angles))


def dot(left, right):
    return jnp.dot(left, right, preferred_element_type=F32)


def dot_nt(left, right):
    return lax.dot_general(left, right, (((1,), (1,)), ((), ())), preferred_element_type=F32)


def dot_tn(left, right):
    return lax.dot_general(left, right, (((0,), (0,)), ((), ())), preferred_element_type=F32)


VMEM = pl.BlockSpec(memory_space=pltpu.VMEM)
SMEM = pl.BlockSpec(memory_space=pltpu.SMEM)
ANY = pl.BlockSpec(memory_space=pl.ANY)
BIG = pltpu.CompilerParams(vmem_limit_bytes=56 * 1024 * 1024)


def line_sums(mine, passed):
    count = lax.axis_size("seq") // 2
    rows = mine.shape[0] // count
    out = []
    for k in range(count):
        part = slice(k * rows, (k + 1) * rows)
        total = mine[part].astype(F32) + passed[part].astype(F32)
        out.append(total.astype(BF) if k else total)
    return out


def line_first(blocks):
    if len(blocks) != 4:
        return [swap(blocks[k], "seq", 2 * k) for k in range(1, len(blocks))]
    return [swap(blocks[1], "seq", 2), swap(blocks[2], "seq", 2)]


def line_second(blocks, first):
    if len(blocks) != 4:
        return []
    return [swap((blocks[3].astype(F32) + first[1].astype(F32)).astype(BF), "seq", 6)]


def line_total(blocks, first, second):
    parts = first[:1] + second if len(blocks) == 4 else first
    total = blocks[0]
    for part in parts:
        total = total + part.astype(F32)
    return total


def line_place(block, seq, count):
    away = block ^ seq
    return (away >> 1) + (away & 1) * (count // 2)


def line_block(place, seq, count):
    half = count // 2
    return seq ^ (2 * place if place < half else 2 * (place - half) + 1)


def line_block_at(spot, seq, count):
    half = count // 2
    return seq ^ (2 * (spot % half) + spot // half)


def line_order(values, seq, count):
    width = values.shape[1] // count
    return jnp.concatenate(
        [
            lax.dynamic_slice_in_dim(values, line_block(m, seq, count) * width, width, 1)
            for m in range(count)
        ],
        axis=1,
    )


def rms_of(values):
    return lax.rsqrt(jnp.mean(values * values, axis=-1, keepdims=True) + EPSILON)


def turn(values, cosine, sine):
    return values * cosine + pltpu.roll(values, values.shape[1] // 2, 1) * sine


def at(block, width):
    return pl.ds(pl.multiple_of(block * width, width), width)


def grouped(refs, counts):
    out, start = [], 0
    for count in counts:
        out.append(refs[start : start + count])
        start += count
    return out


def chunk_of(pieces, c, count):
    if len(pieces) == count:
        return pieces[c][...]
    rows = pieces[0].shape[0] // count
    return pieces[0][c * rows : (c + 1) * rows]


def piece_dot(left, pieces):
    total, row = None, 0
    for ref in pieces:
        rows = ref.shape[0]
        part = dot(left[:, row : row + rows], ref[...])
        total = part if total is None else total + part
        row += rows
    return total


def project_kernel(shape, *refs):
    counts, seqs = shape
    slots, count, chunks = len(counts), sum(counts), max(counts)
    place, rows_ref, gain_ref, valid_ref, cos_ref, sin_ref = refs[:6]
    mine = grouped(refs[6 : 6 + count], counts)
    theirs = grouped(refs[6 + count : 6 + 2 * count], counts)
    kv_mine, kv_theirs = refs[6 + 2 * count : 8 + 2 * count]
    normed_ref, query_ref, shared_ref, line_ref = refs[8 + 2 * count :]
    seq = place[0]
    model = rows_ref.shape[1]
    half = model // 2
    width = model // seqs
    scale = rms_of(rows_ref[...].astype(F32))
    for m in range(seqs):
        block = at(line_block(m, seq, seqs), width)
        to = slice(m * width, (m + 1) * width)
        part = rows_ref[:, block].astype(F32)
        part = (part * scale * gain_ref[:, to]).astype(BF)
        normed_ref[:, block] = part
        line_ref[:, to] = part
    cosine, sine = cos_ref[...], sin_ref[...]
    head = cosine.shape[1]
    left, right = line_ref[:, :half], line_ref[:, half:]
    col = 0
    for i in range(slots):
        total = piece_dot(left, mine[i]) + piece_dot(right, theirs[i])
        for h in range(total.shape[1] // head):
            turned = turn(total[:, h * head : (h + 1) * head], cosine, sine)
            query_ref[:, col : col + head] = turned.astype(BF)
            col += head
    kv = dot(left, kv_mine[...]) + dot(right, kv_theirs[...])
    valid = valid_ref[...]
    shared_ref[:, :head] = (turn(kv[:, :head], cosine, sine) * valid).astype(BF)
    shared_ref[:, head:] = (kv[:, head:] * valid).astype(BF)


def set_bias(place, bias_ref, step):
    @pl.when(step == 0)
    def _():
        toks, keys = bias_ref.shape
        first = place[0] * toks
        query = first + lax.broadcasted_iota(jnp.int32, (toks, keys), 0)
        key = first - WINDOW + lax.broadcasted_iota(jnp.int32, (toks, keys), 1)
        length = place[2]
        away = query - key
        good = (key >= 0) & (key < length) & (away >= 0) & (away < WINDOW) & (query < length)
        bias_ref[...] = jnp.where(good, 0.0, NEGATIVE)


def softmax_rows(place, query, keys, bias):
    head = query.shape[1]
    scores = dot_nt(query, keys) * (head**-0.5) + bias
    grown = jnp.exp(scores - jnp.max(scores, axis=-1, keepdims=True))
    toks = query.shape[0]
    pos = place[0] * toks + lax.broadcasted_iota(jnp.int32, (toks, 1), 0)
    total = jnp.sum(grown, axis=-1, keepdims=True)
    return grown * jnp.where(pos < place[2], 1.0 / total, 0.0)


def attend_kernel(rims, late, place, query_ref, *refs):
    table = refs[: rims + 1]
    out_ref, bias_ref = refs[rims + 1 + late :]
    set_bias(place, bias_ref, pl.program_id(0))
    head = query_ref.shape[1]
    keys = jnp.concatenate([ref[:, :head] for ref in table], axis=0)
    values = jnp.concatenate([ref[:, head:] for ref in table], axis=0)
    probs = softmax_rows(place, query_ref[...], keys, bias_ref[...])
    out_ref[...] = dot(probs.astype(BF), values).astype(BF)


def attend_back_kernel(rims, late, place, query_ref, grad_ref, *refs):
    table = refs[: rims + 1]
    cos_ref, sin_ref = refs[rims + 1 : rims + 3]
    gq_ref, gkv_ref, bias_ref = refs[rims + 3 + late :]
    step = pl.program_id(0)
    set_bias(place, bias_ref, step)

    @pl.when(step == 0)
    def _():
        gkv_ref[...] = jnp.zeros_like(gkv_ref)

    head = query_ref.shape[1]
    scaling = head**-0.5
    keys = jnp.concatenate([ref[:, :head] for ref in table], axis=0)
    values = jnp.concatenate([ref[:, head:] for ref in table], axis=0)
    query, grad = query_ref[...], grad_ref[...]
    probs = softmax_rows(place, query, keys, bias_ref[...])
    grad_probs = dot_nt(grad, values)
    both = probs * grad_probs
    grad_scores = (both - probs * jnp.sum(both, axis=-1, keepdims=True)).astype(BF)
    grad_query = dot(grad_scores, keys) * scaling
    gq_ref[...] = turn(grad_query, cos_ref[...], -sin_ref[...]).astype(BF)
    gkv_ref[:, :head] += dot_tn(grad_scores, query) * scaling
    gkv_ref[:, head:] += dot_tn(probs.astype(BF), grad)


def out_kernel(shape, *refs):
    counts, seqs = shape
    slots, count, chunks = len(counts), sum(counts), max(counts)
    place, att_ref, rows_ref, gain_ref = refs[:4]
    mine = grouped(refs[4 : 4 + count], counts)
    theirs = grouped(refs[4 + count : 4 + 2 * count], counts)
    middle_ref, normed_ref, plain_ref = refs[4 + 2 * count :]
    seq, slot = place[0], place[1]
    model = rows_ref.shape[1]
    half = model // 2
    width = model // seqs
    left, right = att_ref[:, :half], att_ref[:, half:]
    for i in range(slots):
        total = piece_dot(left, mine[i]) + piece_dot(right, theirs[i])
        to = at(slot ^ i, total.shape[1])
        middle_ref[:, to] = rows_ref[:, to].astype(F32) + total
    scale = rms_of(middle_ref[...])
    for m in range(seqs):
        to = at(line_block(m, seq, seqs), width)
        gain = gain_ref[:, m * width : (m + 1) * width]
        normed_ref[:, to] = (middle_ref[:, to] * scale * gain).astype(BF)
        plain_ref[:, to] = att_ref[:, m * width : (m + 1) * width]


def mid_back_kernel(shape, *refs):
    counts, seqs = shape
    slots, count, chunks = len(counts), sum(counts), max(counts)
    place, grad_ref, middle_ref, cot_ref, gain_ref = refs[:5]
    mine = grouped(refs[5 : 5 + count], counts)
    theirs = grouped(refs[5 + count : 5 + 2 * count], counts)
    gmid_ref, gatt_ref, ggain_ref = refs[5 + 2 * count : 8 + 2 * count]
    branch = refs[8 + 2 * count :]
    seq, slot = place[0], place[1]
    model = middle_ref.shape[1]
    half = model // 2
    width = model // seqs
    scale = rms_of(middle_ref[...])
    mean = 0.0
    for m in range(seqs):
        to = at(line_block(m, seq, seqs), width)
        here = slice(m * width, (m + 1) * width)
        grad = grad_ref[:, to]
        unit = middle_ref[:, to] * scale
        ggain_ref[:, to] = jnp.sum(grad * unit, axis=0, keepdims=True)
        scaled = grad * gain_ref[:, here]
        gmid_ref[:, to] = scaled
        mean = mean + jnp.sum(scaled * unit, axis=1, keepdims=True)
    mean = mean * (1.0 / model)
    gmid_ref[...] = cot_ref[...].astype(F32) + scale * (
        gmid_ref[...] - middle_ref[...] * (scale * mean)
    )
    out_cols = model // slots
    for i in range(slots):
        branch[i][...] = gmid_ref[:, at(slot ^ i, out_cols)].astype(BF)
    for pieces, start in ((mine, 0), (theirs, half)):
        row = start
        for c in range(chunks):
            rows = half // chunks
            total = dot_nt(branch[0][...], chunk_of(pieces[0], c, chunks))
            for i in range(1, slots):
                total = total + dot_nt(branch[i][...], chunk_of(pieces[i], c, chunks))
            gatt_ref[:, row : row + rows] = total.astype(BF)
            row += rows


def input_back_kernel(shape, *refs):
    counts, seqs = shape
    slots, count, chunks = len(counts), sum(counts), max(counts)
    place, gq_ref, gkv_ref, rows_ref, gmid_ref, gain_ref = refs[:6]
    mine = grouped(refs[6 : 6 + count], counts)
    theirs = grouped(refs[6 + count : 6 + 2 * count], counts)
    kv_mine, kv_theirs = refs[6 + 2 * count : 8 + 2 * count]
    out_ref, ggain_ref, scaled_ref = refs[8 + 2 * count :]
    seq = place[0]
    model = rows_ref.shape[1]
    half = model // 2
    width = model // seqs
    cols = model // slots
    rows_in = rows_ref[...].astype(F32)
    scale = rms_of(rows_in)
    mean = 0.0
    for pieces, kv_ref, start in ((mine, kv_mine, 0), (theirs, kv_theirs, half)):
        row = 0
        for c in range(chunks):
            rows = half // chunks
            total = dot_nt(gkv_ref[...], kv_ref[row : row + rows])
            for i in range(slots):
                total = total + dot_nt(
                    gq_ref[:, i * cols : (i + 1) * cols], chunk_of(pieces[i], c, chunks)
                )
            for b in range(rows // width):
                m = (start + row) // width + b
                here = slice(m * width, (m + 1) * width)
                to = at(line_block(m, seq, seqs), width)
                grad = total[:, b * width : (b + 1) * width]
                unit = rows_ref[:, to].astype(F32) * scale
                ggain_ref[:, to] = jnp.sum(grad * unit, axis=0, keepdims=True)
                scaled = grad * gain_ref[:, here]
                scaled_ref[:, to] = scaled
                mean = mean + jnp.sum(scaled * unit, axis=1, keepdims=True)
            row += rows
    mean = mean * (1.0 / model)
    out_ref[...] = (
        gmid_ref[...] + scale * (scaled_ref[...] - rows_in * (scale * mean))
    ).astype(BF)


def share_kernel(slots, seqs, place, gate_ref, up_ref, out_ref):
    piece = gate_ref.shape[1] // (slots * seqs)
    width = piece * seqs
    for s in range(slots):

        @pl.when(place[1] == s)
        def _():
            for n, ref in enumerate((gate_ref, up_ref)):
                parts = [
                    ref[:, (q * slots + s) * piece : (q * slots + s + 1) * piece]
                    for q in range(seqs)
                ]
                out_ref[:, n * width : (n + 1) * width] = jnp.concatenate(parts, axis=1)


def parts_product(left, right):
    total, block, row = None, 0, 0
    for ref in left:
        rows = ref.shape[0]
        part = dot_tn(ref[...], right[block][row : row + rows])
        total = part if total is None else total + part
        row += rows
        if row == right[block].shape[0]:
            block, row = block + 1, 0
    return total


def line_grads_kernel(count, slots, place, *refs):
    normed, attended = refs[:count], refs[count : 2 * count]
    traded, branch = refs[2 * count : 2 * count + slots], refs[2 * count + slots :][:slots]
    gain_ref, out_ref = refs[2 * count + 2 * slots], refs[-1]
    first = parts_product(normed, traded)
    second = parts_product(attended, branch)
    start = first.shape[1]
    end = start + second.shape[1]
    out_ref[:, :start] = first.astype(BF)
    out_ref[:, start:end] = second.astype(BF)
    out_ref[:, end:] = gain_ref[...]


def cut_store(total, outs):
    row = 0
    for ref in outs:
        rows = ref.shape[0]
        ref[...] = total[row : row + rows].astype(BF)
        row += rows


def gate_kernel(count, *refs):
    tokens = refs[:count]
    wgate_ref, wup_ref, all_ref, gate_ref, up_ref, hidden_ref = refs[count:]

    @pl.when(pl.program_id(0) == 0)
    def _():
        row = 0
        for ref in tokens:
            all_ref[row : row + ref.shape[0]] = ref[...]
            row += ref.shape[0]

    tile = wgate_ref.shape[1]
    both = dot(all_ref[...], jnp.concatenate([wgate_ref[...], wup_ref[...]], axis=1))
    gate, up = both[:, :tile], both[:, tile:]
    gate_ref[...] = gate.astype(BF)
    up_ref[...] = up.astype(BF)
    hidden_ref[...] = (gate * jax.nn.sigmoid(gate) * up).astype(BF)


def rows_kernel(transposed, late, left_ref, right_ref, *refs):
    right = right_ref[...]
    total = dot_nt(left_ref[...], right) if transposed else dot(left_ref[...], right)
    cut_store(total, refs[late:])


def unline_kernel(seqs, place, *refs):
    out_ref = refs[seqs]
    for m in range(seqs):
        rows = refs[m].shape[0]
        to = pl.ds(pl.multiple_of(line_block(m, place[0], seqs) * rows, rows), rows)
        out_ref[to] = refs[m][...]


def unshare_kernel(slots, seqs, part_ref, gate_ref, up_ref):
    width = part_ref.shape[2] // 2
    piece = width // seqs
    for n, ref in enumerate((gate_ref, up_ref)):
        parts = [
            part_ref[s, :, n * width + q * piece : n * width + (q + 1) * piece]
            for q in range(seqs)
            for s in range(slots)
        ]
        ref[...] = jnp.concatenate(parts, axis=1).astype(F32)


def tie(value, *after):
    return pl.pallas_call(
        lambda *refs: None,
        out_shape=jax.ShapeDtypeStruct(value.shape, value.dtype),
        in_specs=[ANY] * (1 + len(after)),
        out_specs=ANY,
        input_output_aliases={0: 0},
    )(value, *after)


def fence(values, after):
    count = len(values)
    return list(
        pl.pallas_call(
            lambda *refs: None,
            out_shape=[jax.ShapeDtypeStruct(value.shape, value.dtype) for value in values],
            in_specs=[ANY] * (count + len(after)),
            out_specs=[ANY] * count,
            input_output_aliases={k: k for k in range(count)},
        )(*values, *after)
    )


class Flow:
    def __init__(self):
        self.now = []

    def at(self, *values):
        self.now = list(values)

    def go(self, *values):
        kept = {id(value) for value in values}
        return fence(list(values), [value for value in self.now if id(value) not in kept])


def call(kernel, inputs, late, out_shape, in_specs=None, scratch=()):
    count = len(inputs)
    single = not isinstance(out_shape, (tuple, list))

    def run(*refs):
        kernel(*refs[:count], *refs[count + len(late) :])

    return pl.pallas_call(
        run,
        out_shape=out_shape,
        in_specs=[SMEM] + [VMEM] * (count - 1) + [ANY] * len(late),
        out_specs=VMEM if single else (VMEM,) * len(out_shape),
        scratch_shapes=list(scratch),
        compiler_params=BIG,
    )(*inputs, *late)


def shape_of(rows, cols, kind):
    return jax.ShapeDtypeStruct((rows, cols), kind)


def shards(
    rows_in,
    lengths,
    norm1_gain,
    w_query,
    w_key,
    w_value,
    w_out,
    norm2_gain,
    w_gate,
    w_up,
    w_down,
    rows_cot,
    kv_cot,
):
    slots = lax.axis_size("slot")
    seqs = lax.axis_size("seq")
    slot = lax.axis_index("slot")
    seq = lax.axis_index("seq")
    tok_count = rows_in.shape[1]
    model = rows_in.shape[2]
    head_width = w_key.shape[1]
    head_count = w_query.shape[1] // head_width
    hop_count = WINDOW // tok_count
    key_count = WINDOW + tok_count
    rows_dev = w_query.shape[0]
    cols_slot = w_query.shape[1] // slots
    out_slot = w_out.shape[1] // slots
    hidden_all = w_gate.shape[1]
    piece = hidden_all // (slots * seqs)
    hidden_slot = piece * seqs
    half = model // 2
    extra = 16
    place = jnp.stack([seq, slot, lengths[0]]).astype(jnp.int32)
    rows_own, cot_own = rows_in[0], rows_cot[0]

    first_row = seq * tok_count
    query_pos = first_row + jnp.arange(tok_count, dtype=jnp.int32)
    row_valid = (query_pos < lengths[0]).astype(F32)[:, None]
    flow = Flow()

    gains = jnp.stack([norm1_gain, norm2_gain], axis=0)
    pack = jnp.concatenate(
        [lax.dynamic_slice_in_dim(w_query, slot * cols_slot, cols_slot, 1), w_key, w_value], axis=1
    )
    gains = jnp.pad(gains, ((0, extra - 2), (cols_slot, pack.shape[1] - cols_slot - rows_dev)))
    pack = jnp.concatenate([pack, gains], axis=0)
    pack_near = line_near(pack)
    cot_near = gather_near(cot_own * row_valid.astype(BF))
    gu_share = call(
        functools.partial(share_kernel, slots, seqs),
        (place, w_gate, w_up),
        (),
        shape_of(rows_dev, 2 * hidden_slot, BF),
    )
    out_share = lax.dynamic_slice_in_dim(w_out, slot * out_slot, out_slot, 1)
    down_share = lax.dynamic_slice_in_dim(w_down, slot * piece, piece, 0)
    flow.at(*pack_near[1:], *cot_near[1:], gu_share)

    *pack_near[1:], out_share = flow.go(*pack_near[1:], out_share)
    *cot_near[1:], down_share = flow.go(*cot_near[1:], down_share)
    pack_far = line_far(pack_near)
    out_near = line_near(out_share)
    cot_far = gather_far(cot_near)
    flow.at(*pack_far, *out_near[1:], *cot_far)

    pack_line = line_all(pack_near, pack_far)
    query_line = jnp.concatenate([block[:rows_dev, :cols_slot] for block in pack_line], axis=0)
    kv_gain = jnp.concatenate([block[:, cols_slot:] for block in pack_line], axis=0)
    query_line, kv_gain, out_near[-1], gu_share = flow.go(
        query_line, kv_gain, out_near[-1], gu_share
    )
    gu_w = lax.all_gather(gu_share, "seq", axis=0, tiled=True)
    down_w = lax.all_gather(down_share, "seq", axis=0, tiled=True)
    query_near = gather_near(query_line)
    query_other = [swap(query_line, "seq", 1)]
    kv_other = swap(kv_gain, "seq", 1)
    out_far = line_far(out_near)
    flow.at(*query_near[1:], query_other[0], kv_other, *out_far)

    query_near[1:] = flow.go(*query_near[1:])
    query_far = gather_far(query_near)
    query_other += [swap(part, "seq", 1) for part in query_near[1:]]
    flow.at(*query_far, *query_other[1:])

    *query_far, out_line = flow.go(
        *query_far, jnp.concatenate(line_all(out_near, out_far), axis=0)
    )
    query_other += [swap(part, "seq", 1) for part in query_far]
    query_w = query_near + query_far + query_other
    out_near = gather_near(out_line)
    flow.at(*query_w[len(query_near) :])
    kv_w, gain_line = [], []
    for part in (kv_gain, kv_other):
        part = part.reshape(seqs // 2, rows_dev + extra, -1)
        kv_w.append(part[:, :rows_dev].reshape(half, -1))
        gain_line.append(part[:, rows_dev : rows_dev + 2, :rows_dev])
    gain_line = jnp.concatenate(gain_line, axis=0).transpose(1, 0, 2).reshape(2, 1, model)
    gain_line = gain_line.astype(F32)
    gain_one, gain_two = gain_line[0], gain_line[1]
    shape = ((1, 1, 1, 2) if slots == 4 else (1,) * slots, seqs)

    cosine, sine = rope_tables(query_pos, head_width)
    cosine = jnp.concatenate([cosine, cosine], axis=1)
    sine = jnp.concatenate([-sine, sine], axis=1)
    normed, queries, shared = call(
        functools.partial(project_kernel, shape),
        (place, rows_own, gain_one, row_valid, cosine, sine, *query_w, *kv_w),
        (),
        (
            shape_of(tok_count, model, BF),
            shape_of(tok_count, head_count * head_width, BF),
            shape_of(tok_count, 2 * head_width, BF),
        ),
        scratch=[pltpu.VMEM((tok_count, model), BF)],
    )
    out_other = [swap(out_near[0], "seq", 1)]
    table = [shifted(shared, "seq", hop) for hop in range(hop_count, 0, -1)] + [shared]
    flow.at(*table[:-1], out_other[0], *out_near[1:])

    slot_heads = head_count // slots
    block_heads = rows_dev // head_width

    def own_col(p, place):
        return (0, p)

    def line_col(p, place):
        head = (place[1] ^ (p // slot_heads)) * slot_heads + p % slot_heads
        spot = line_place(head // block_heads, place[0], seqs)
        return (0, spot * block_heads + head % block_heads)

    def fixed(p, place):
        return (0, 0)

    head_own = pl.BlockSpec((tok_count, head_width), own_col)
    head_line = pl.BlockSpec((tok_count, head_width), line_col)
    table_spec = [pl.BlockSpec((tok_count, 2 * head_width), fixed)] * (hop_count + 1)
    angle_spec = [pl.BlockSpec((tok_count, head_width), fixed)] * 2
    bias_scratch = [pltpu.VMEM((tok_count, key_count), F32)]
    out_near[1:] = flow.go(*out_near[1:])
    out_far = gather_far(out_near)
    out_other += [swap(part, "seq", 1) for part in out_near[1:]]
    late = out_near[1:]
    attended = pl.pallas_call(
        functools.partial(attend_kernel, hop_count, len(late)),
        out_shape=shape_of(tok_count, head_count * head_width, BF),
        grid_spec=pltpu.PrefetchScalarGridSpec(
            num_scalar_prefetch=1,
            grid=(head_count,),
            in_specs=[head_own] + table_spec + [ANY] * len(late),
            out_specs=head_line,
            scratch_shapes=bias_scratch,
        ),
        compiler_params=BIG,
    )(place, queries, *table, *late)
    flow.at(*out_far, *out_other[1:], attended)
    if out_far:
        out_far = flow.go(*out_far)
    out_other += [swap(part, "seq", 1) for part in out_far]
    out_w = out_near + out_far + out_other
    middle, normed_two, attended = call(
        functools.partial(out_kernel, shape),
        (place, attended, rows_own, gain_two, *out_w),
        (),
        (
            shape_of(tok_count, model, F32),
            shape_of(tok_count, model, BF),
            shape_of(tok_count, model, BF),
        ),
    )

    normed_two_near = gather_near(normed_two)
    cot_rows = jnp.concatenate(cot_near + cot_far, axis=0)
    flow.at(*normed_two_near[1:], cot_rows)
    normed_two_near[1:] = flow.go(*normed_two_near[1:])
    normed_two_parts = normed_two_near + gather_far(normed_two_near)
    flow.at(*normed_two_parts[len(normed_two_near) - 1 :])

    normed_near = gather_near(tie(normed, *normed_two_parts[slots - 1 :]))
    tokens = slots * tok_count
    tile = 128
    if hidden_slot % tile == 0:
        steps = hidden_slot // tile
        part_spec = pl.BlockSpec((tokens, tile), lambda j: (0, j))
        normed_two_all, gate_out, up_out, hidden = pl.pallas_call(
            functools.partial(gate_kernel, len(normed_two_parts)),
            out_shape=(shape_of(tokens, model, BF),) + (shape_of(tokens, hidden_slot, BF),) * 3,
            grid=(steps,),
            in_specs=[pl.BlockSpec(part.shape, lambda j: (0, 0)) for part in normed_two_parts]
            + [
                pl.BlockSpec((model, tile), lambda j: (0, j)),
                pl.BlockSpec((model, tile), lambda j: (0, steps + j)),
            ],
            out_specs=(pl.BlockSpec((tokens, model), lambda j: (0, 0)),) + (part_spec,) * 3,
            compiler_params=BIG,
        )(*normed_two_parts, gu_w, gu_w)
        gate_out, up_out = gate_out.astype(F32), up_out.astype(F32)
    else:
        normed_two_all = jnp.concatenate(normed_two_parts, axis=0)
        gu_out = dot(normed_two_all, gu_w)
        gate_out, up_out = gu_out[:, :hidden_slot], gu_out[:, hidden_slot:]
        hidden = (gate_out * jax.nn.sigmoid(gate_out) * up_out).astype(BF)
    sig_gate = jax.nn.sigmoid(gate_out)
    cot_rows = tie(cot_rows, *normed_near[1:], hidden)
    grad_down = dot_tn(hidden, cot_rows).astype(BF)
    own_down = lax.psum_scatter(grad_down, "seq", scatter_dimension=0, tiled=True)
    *normed_near[1:], attended = fence([*normed_near[1:], attended], [cot_rows])
    normed_all = normed_near + gather_far(normed_near)
    attended_near = gather_near(attended)

    grad_hidden = dot_nt(cot_rows, down_w)
    grad_gate = grad_hidden * up_out * sig_gate * (1.0 + gate_out * (1.0 - sig_gate))
    grad_up = grad_hidden * gate_out * sig_gate
    grad_gu = jnp.concatenate([grad_gate.astype(BF), grad_up.astype(BF)], axis=1)
    grad_gate_w = dot_tn(normed_two_all, grad_gu[:, :hidden_slot]).astype(BF)
    grad_gu = tie(grad_gu, *normed_all[slots - 1 :], *attended_near[1:], grad_gate_w)
    half_tok = tok_count // 2
    cut_rows = [tok_count] + [half_tok] * 6 if slots == 4 else [tok_count] * slots

    def cut_product(left, right, transposed, late):
        width = 512
        depth = left.shape[1]
        right_spec = (
            pl.BlockSpec((width, depth), lambda j: (j, 0))
            if transposed
            else pl.BlockSpec((depth, width), lambda j: (0, j))
        )
        return list(
            pl.pallas_call(
                functools.partial(rows_kernel, transposed, len(late)),
                out_shape=[shape_of(rows, model, BF) for rows in cut_rows],
                grid=(model // width,),
                in_specs=[pl.BlockSpec(left.shape, lambda j: (0, 0)), right_spec]
                + [ANY] * len(late),
                out_specs=[pl.BlockSpec((rows, width), lambda j: (0, j)) for rows in cut_rows],
                compiler_params=BIG,
            )(left, right, *late)
        )

    attended_near[1:] = fence(attended_near[1:], [grad_gu])
    attended_all = attended_near + gather_far(attended_near)
    grad_parts = cut_product(grad_gu, gu_w, True, ())
    if slots == 4:
        grad_parts[5:] = fence(
            grad_parts[5:], attended_all[slots - 1 :]
        )
    passed = scatter_pass(grad_parts)
    down_parts = cut_product(tie(hidden, grad_parts[0]), down_w, False, ())
    if slots == 4:
        *passed, grad_parts[2], grad_parts[3], grad_gu = fence(
            [*passed, grad_parts[2], grad_parts[3], grad_gu], [down_parts[0]]
        )
    near = scatter_near(grad_parts)
    far = scatter_far(grad_parts, passed)
    grad_gate_w = tie(grad_gate_w, own_down, *passed)
    own_gate = lax.psum_scatter(grad_gate_w, "seq", scatter_dimension=0, tiled=True)
    grad_up_w = dot_tn(normed_two_all, grad_gu[:, hidden_slot:]).astype(BF)
    grad_normed_two = scatter_total(grad_parts, near, far)
    down_parts[-1] = tie(down_parts[-1], grad_normed_two)
    down_passed = scatter_pass(
        [*down_parts[:-2], tie(down_parts[-2], down_parts[-1]), down_parts[-1]]
    )

    grad_middle, grad_attended, grad_gain_two, *branch = call(
        functools.partial(mid_back_kernel, shape),
        (place, grad_normed_two, middle, cot_own, gain_two, *out_w),
        (grad_up_w, *down_passed),
        (
            shape_of(tok_count, model, F32),
            shape_of(tok_count, head_count * head_width, BF),
            shape_of(1, model, F32),
        )
        + (shape_of(tok_count, out_slot, BF),) * slots,
    )
    branch_all = trade_slot(branch)
    own_down_near = gather_near(tie(own_down, branch[0]))

    grad_query, grad_table = pl.pallas_call(
        functools.partial(attend_back_kernel, hop_count, 0),
        out_shape=(
            shape_of(tok_count, head_count * head_width, BF),
            shape_of(key_count, 2 * head_width, F32),
        ),
        grid_spec=pltpu.PrefetchScalarGridSpec(
            num_scalar_prefetch=1,
            grid=(head_count,),
            in_specs=[head_own, head_line] + table_spec + angle_spec,
            out_specs=(head_own, pl.BlockSpec((key_count, 2 * head_width), fixed)),
            scratch_shapes=bias_scratch,
        ),
        compiler_params=BIG,
    )(place, queries, grad_attended, *table, cosine, sine)
    grad_table, *down_passed = fence([grad_table, *down_passed], branch_all[1:])
    grad_up_w = tie(grad_up_w, own_gate, grad_table)
    own_up = lax.psum_scatter(grad_up_w, "seq", scatter_dimension=0, tiled=True)
    own_grad = grad_table[WINDOW:] + kv_cot[0].astype(F32)
    for hop in range(1, hop_count + 1):
        lower = (hop_count - hop) * tok_count
        own_grad = own_grad + shifted(
            grad_table[lower : lower + tok_count].astype(BF), "seq", -hop
        ).astype(F32)
    own_grad = own_grad * row_valid
    grad_key = own_grad[:, :head_width]
    grad_key = grad_key * cosine - jnp.roll(grad_key, head_width // 2, axis=1) * sine
    grad_kv = jnp.concatenate([grad_key, own_grad[:, head_width:]], axis=1).astype(BF)
    grad_kv, down_parts[2], *own_down_near[1:] = fence(
        [grad_kv, down_parts[2], *own_down_near[1:]], []
    )
    down_near = scatter_near(
        [*down_parts[:3], tie(down_parts[3], down_parts[2]), *down_parts[4:]]
        if slots == 4
        else down_parts
    )
    traded = [
        jnp.concatenate([grad_query[:, j * cols_slot : (j + 1) * cols_slot], grad_kv], axis=1)
        for j in range(slots)
    ]
    late = traded
    traded = trade_slot(traded)
    grad_inputs, grad_gain_one = call(
        functools.partial(input_back_kernel, shape),
        (place, grad_query, grad_kv, rows_own, grad_middle, gain_one, *query_w, *kv_w),
        late,
        (shape_of(tok_count, model, BF), shape_of(1, model, F32)),
        scratch=[pltpu.VMEM((tok_count, model), F32)],
    )
    gain_grads = jnp.concatenate([grad_gain_one, grad_gain_two], axis=0).astype(BF)
    gain_grads = jnp.pad(gain_grads.T, ((0, 0), (0, head_width - 2)))
    late = [grad_inputs, *traded[1:], *down_near]
    gain_grads, down_parts[1], *down_passed = fence(
        [gain_grads, down_parts[1], *down_passed], late
    )
    own_down_near[1:] = fence(own_down_near[1:], [gain_grads])
    down_far = scatter_far(down_parts, down_passed)
    own_down_all = own_down_near + gather_far(own_down_near)
    width_all = traded[0].shape[1] + branch_all[0].shape[1] + head_width
    places = seqs // 2

    def line_grads(start, late):
        def columns(m, place):
            return (0, line_block_at(start + m, place[0], seqs))

        def rows(m, place):
            return (line_block_at(start + m, place[0], seqs), 0)

        return pl.pallas_call(
            functools.partial(line_grads_kernel, len(normed_all), slots),
            out_shape=shape_of(half, width_all, BF),
            grid_spec=pltpu.PrefetchScalarGridSpec(
                num_scalar_prefetch=1,
                grid=(places,),
                in_specs=[
                    pl.BlockSpec((part.shape[0], rows_dev), columns)
                    for part in normed_all + attended_all
                ]
                + [pl.BlockSpec(part.shape, fixed) for part in traded + branch_all]
                + [pl.BlockSpec((rows_dev, head_width), rows)]
                + [ANY] * len(late),
                out_specs=pl.BlockSpec((rows_dev, width_all), lambda m, place: (m, 0)),
            ),
            compiler_params=BIG,
        )(place, *normed_all, *attended_all, *traded, *branch_all, gain_grads, *late)

    mine = line_grads(0, ())
    theirs = line_grads(places, (mine,))
    passed = swap(theirs, "seq", 1)
    line = line_sums(mine, passed)
    first = line_first(line)
    down_total = scatter_total(down_parts, down_near, down_far)
    result = (middle + down_total * row_valid).astype(BF)
    second = line_second(line, first)
    own_hidden = jnp.concatenate([own_gate, own_up], axis=1)
    hidden_parts = lax.all_gather(own_hidden, "slot", axis=0)
    own = line_total(line, first, second)
    kv_end = cols_slot + 2 * head_width
    shared_out = jnp.concatenate([own[:, :cols_slot], own[:, kv_end:]], axis=1).astype(BF)
    shared_near = gather_near(shared_out)
    row_tile = 32

    gate_grad, up_grad = pl.pallas_call(
        functools.partial(unshare_kernel, slots, seqs),
        out_shape=(shape_of(rows_dev, hidden_all, F32),) * 2,
        grid=(rows_dev // row_tile,),
        in_specs=[pl.BlockSpec((slots, row_tile, 2 * hidden_slot), lambda r: (0, r, 0))],
        out_specs=(pl.BlockSpec((row_tile, hidden_all), lambda r: (r, 0)),) * 2,
        compiler_params=BIG,
    )(hidden_parts)
    all_own = jnp.concatenate(shared_near + gather_far(shared_near), axis=0)
    all_own = all_own.reshape(slots, rows_dev, -1)
    all_own = jnp.stack(
        [lax.dynamic_index_in_dim(all_own, slot ^ j, 0, keepdims=False) for j in range(slots)]
    )

    def by_slot(parts):
        parts = jnp.concatenate(parts, axis=0).reshape(slots, -1, parts[0].shape[1])
        return jnp.stack(
            [lax.dynamic_index_in_dim(parts, slot ^ j, 0, keepdims=False) for j in range(slots)]
        )

    def slot_columns(parts):
        return parts.transpose(1, 0, 2).reshape(rows_dev, -1).astype(F32)

    query_grad = slot_columns(all_own[:, :, :cols_slot])
    out_grad_w = slot_columns(all_own[:, :, cols_slot : cols_slot + out_slot])
    gain_total = jnp.sum(all_own[:, :, cols_slot + out_slot :][:, :, :2].astype(F32), axis=0)
    down_grad = by_slot(own_down_all).reshape(slots * piece, model).astype(F32)
    return (
        result[None],
        shared[None],
        grad_inputs[None],
        gain_total[:, 0],
        query_grad,
        own[:, cols_slot : cols_slot + head_width].astype(F32),
        own[:, cols_slot + head_width : kv_end].astype(F32),
        out_grad_w,
        gain_total[:, 1],
        gate_grad,
        up_grad,
        down_grad,
    )


def solution(mesh):
    placed = (
        P("slot", "seq", None),
        P("slot"),
        P("seq"),
        P("seq", None),
        P("seq", None),
        P("seq", None),
        P("seq", None),
        P("seq"),
        P("seq", None),
        P("seq", None),
        P("seq", None),
        P("slot", "seq", None),
        P("slot", "seq", None),
    )
    return jax.shard_map(
        shards,
        mesh=mesh,
        in_specs=placed,
        out_specs=(
            P("slot", "seq", None),
            P("slot", "seq", None),
            P("slot", "seq", None),
            P("seq"),
            P("seq", None),
            P("seq", None),
            P("seq", None),
            P("seq", None),
            P("seq"),
            P("seq", None),
            P("seq", None),
            P("seq", None),
        ),
        check_vma=False,
    )
```

```python
import functools

import jax
import jax.numpy as jnp
from jax import lax
from jax.experimental import pallas as pl
from jax.experimental.pallas import tpu as pltpu
from jax.sharding import PartitionSpec as P

WINDOW = 512


EPSILON = 1e-05
THETA = 10000.0
NEGATIVE = -1e30
BF = jnp.bfloat16
F32 = jnp.float32


def swap(block, axis, mask):
    return lax.ppermute(block, axis, [(i, i ^ mask) for i in range(lax.axis_size(axis))])


def gather_near(block):
    count = lax.axis_size("slot")
    if count != 4:
        return [block] + [swap(block, "slot", j) for j in range(1, count)]
    return [block, swap(block, "slot", 1), swap(block, "slot", 2)]


def gather_far(near):
    if lax.axis_size("slot") != 4:
        return []
    half = near[0].shape[0] // 2
    return [swap(near[1][:half], "slot", 2), swap(near[2][half:], "slot", 1)]


def scatter_pass(parts):
    if lax.axis_size("slot") != 4:
        return []
    return [swap(parts[5], "slot", 2), swap(parts[6], "slot", 1)]


def scatter_near(parts):
    if lax.axis_size("slot") != 4:
        return [swap(parts[j], "slot", j) for j in range(1, len(parts))]
    return [swap(parts[2], "slot", 1), swap(parts[3], "slot", 2)]


def scatter_far(parts, passed):
    if lax.axis_size("slot") != 4:
        return []
    low, high = passed
    return [
        swap((parts[1].astype(F32) + low.astype(F32)).astype(BF), "slot", 1),
        swap((parts[4].astype(F32) + high.astype(F32)).astype(BF), "slot", 2),
    ]


def scatter_total(parts, near, far):
    own = parts[0].astype(F32)
    if lax.axis_size("slot") != 4:
        for part in near:
            own = own + part.astype(F32)
        return own
    first = jnp.concatenate([far[0], near[0]], axis=0).astype(F32)
    second = jnp.concatenate([near[1], far[1]], axis=0).astype(F32)
    return own + first + second


def trade_slot(blocks):
    return [blocks[0]] + [swap(blocks[j], "slot", j) for j in range(1, len(blocks))]


def line_near(block):
    count = lax.axis_size("seq")
    if count != 8:
        return [block] + [swap(block, "seq", j) for j in range(2, count, 2)]
    return [block, swap(block, "seq", 2), swap(block, "seq", 6)]


def line_far(near):
    if lax.axis_size("seq") != 8:
        return []
    return [swap(near[2], "seq", 2)]


def line_all(near, far):
    return near[:2] + far + near[2:]


def shifted(block, axis, distance):
    devices = range(lax.axis_size(axis))
    route = [(i - distance, i) for i in devices if i - distance in devices]
    return lax.ppermute(block, axis, route)


def rope_tables(positions, head_width):
    half_width = head_width // 2
    exponent = jnp.arange(half_width, dtype=jnp.float32) * (2.0 / head_width)
    frequency = THETA ** (-exponent)
    angles = positions.astype(jnp.float32)[:, None] * frequency[None, :]
    return (jnp.cos(angles), jnp.sin(angles))


def dot(left, right):
    return jnp.dot(left, right, preferred_element_type=F32)


def dot_nt(left, right):
    return lax.dot_general(left, right, (((1,), (1,)), ((), ())), preferred_element_type=F32)


def dot_tn(left, right):
    return lax.dot_general(left, right, (((0,), (0,)), ((), ())), preferred_element_type=F32)


VMEM = pl.BlockSpec(memory_space=pltpu.VMEM)
SMEM = pl.BlockSpec(memory_space=pltpu.SMEM)
ANY = pl.BlockSpec(memory_space=pl.ANY)
BIG = pltpu.CompilerParams(vmem_limit_bytes=56 * 1024 * 1024)


def line_sums(mine, passed):
    count = lax.axis_size("seq") // 2
    rows = mine.shape[0] // count
    out = []
    for k in range(count):
        part = slice(k * rows, (k + 1) * rows)
        total = mine[part].astype(F32) + passed[part].astype(F32)
        out.append(total.astype(BF) if k else total)
    return out


def line_first(blocks):
    if len(blocks) != 4:
        return [swap(blocks[k], "seq", 2 * k) for k in range(1, len(blocks))]
    return [swap(blocks[1], "seq", 2), swap(blocks[2], "seq", 2)]


def line_second(blocks, first):
    if len(blocks) != 4:
        return []
    return [swap((blocks[3].astype(F32) + first[1].astype(F32)).astype(BF), "seq", 6)]


def line_total(blocks, first, second):
    parts = first[:1] + second if len(blocks) == 4 else first
    total = blocks[0]
    for part in parts:
        total = total + part.astype(F32)
    return total


def line_place(block, seq, count):
    away = block ^ seq
    return (away >> 1) + (away & 1) * (count // 2)


def line_block(place, seq, count):
    half = count // 2
    return seq ^ (2 * place if place < half else 2 * (place - half) + 1)


def line_block_at(spot, seq, count):
    half = count // 2
    return seq ^ (2 * (spot % half) + spot // half)


def line_order(values, seq, count):
    width = values.shape[1] // count
    return jnp.concatenate(
        [
            lax.dynamic_slice_in_dim(values, line_block(m, seq, count) * width, width, 1)
            for m in range(count)
        ],
        axis=1,
    )


def rms_of(values):
    return lax.rsqrt(jnp.mean(values * values, axis=-1, keepdims=True) + EPSILON)


def turn(values, cosine, sine):
    return values * cosine + pltpu.roll(values, values.shape[1] // 2, 1) * sine


def at(block, width):
    return pl.ds(pl.multiple_of(block * width, width), width)


def grouped(refs, counts):
    out, start = [], 0
    for count in counts:
        out.append(refs[start : start + count])
        start += count
    return out


def chunk_of(pieces, c, count):
    if len(pieces) == count:
        return pieces[c][...]
    rows = pieces[0].shape[0] // count
    return pieces[0][c * rows : (c + 1) * rows]


def piece_dot(left, pieces):
    total, row = None, 0
    for ref in pieces:
        rows = ref.shape[0]
        part = dot(left[:, row : row + rows], ref[...])
        total = part if total is None else total + part
        row += rows
    return total


def project_kernel(shape, *refs):
    counts, seqs = shape
    slots, count, chunks = len(counts), sum(counts), max(counts)
    place, rows_ref, gain_ref, valid_ref, cos_ref, sin_ref = refs[:6]
    mine = grouped(refs[6 : 6 + count], counts)
    theirs = grouped(refs[6 + count : 6 + 2 * count], counts)
    kv_mine, kv_theirs = refs[6 + 2 * count : 8 + 2 * count]
    normed_ref, query_ref, shared_ref, line_ref = refs[8 + 2 * count :]
    seq = place[0]
    model = rows_ref.shape[1]
    half = model // 2
    width = model // seqs
    scale = rms_of(rows_ref[...].astype(F32))
    for m in range(seqs):
        block = at(line_block(m, seq, seqs), width)
        to = slice(m * width, (m + 1) * width)
        part = rows_ref[:, block].astype(F32)
        part = (part * scale * gain_ref[:, to]).astype(BF)
        normed_ref[:, block] = part
        line_ref[:, to] = part
    cosine, sine = cos_ref[...], sin_ref[...]
    head = cosine.shape[1]
    left, right = line_ref[:, :half], line_ref[:, half:]
    col = 0
    for i in range(slots):
        total = piece_dot(left, mine[i]) + piece_dot(right, theirs[i])
        for h in range(total.shape[1] // head):
            turned = turn(total[:, h * head : (h + 1) * head], cosine, sine)
            query_ref[:, col : col + head] = turned.astype(BF)
            col += head
    kv = dot(left, kv_mine[...]) + dot(right, kv_theirs[...])
    valid = valid_ref[...]
    shared_ref[:, :head] = (turn(kv[:, :head], cosine, sine) * valid).astype(BF)
    shared_ref[:, head:] = (kv[:, head:] * valid).astype(BF)


def set_bias(place, bias_ref, step):
    @pl.when(step == 0)
    def _():
        toks, keys = bias_ref.shape
        first = place[0] * toks
        query = first + lax.broadcasted_iota(jnp.int32, (toks, keys), 0)
        key = first - WINDOW + lax.broadcasted_iota(jnp.int32, (toks, keys), 1)
        length = place[2]
        away = query - key
        good = (key >= 0) & (key < length) & (away >= 0) & (away < WINDOW) & (query < length)
        bias_ref[...] = jnp.where(good, 0.0, NEGATIVE)


def softmax_rows(place, query, keys, bias):
    head = query.shape[1]
    scores = dot_nt(query, keys) * (head**-0.5) + bias
    grown = jnp.exp(scores - jnp.max(scores, axis=-1, keepdims=True))
    toks = query.shape[0]
    pos = place[0] * toks + lax.broadcasted_iota(jnp.int32, (toks, 1), 0)
    total = jnp.sum(grown, axis=-1, keepdims=True)
    return grown * jnp.where(pos < place[2], 1.0 / total, 0.0)


def attend_kernel(rims, late, place, query_ref, *refs):
    table = refs[: rims + 1]
    out_ref, bias_ref = refs[rims + 1 + late :]
    set_bias(place, bias_ref, pl.program_id(0))
    head = query_ref.shape[1]
    keys = jnp.concatenate([ref[:, :head] for ref in table], axis=0)
    values = jnp.concatenate([ref[:, head:] for ref in table], axis=0)
    probs = softmax_rows(place, query_ref[...], keys, bias_ref[...])
    out_ref[...] = dot(probs.astype(BF), values).astype(BF)


def attend_back_kernel(rims, late, place, query_ref, grad_ref, *refs):
    table = refs[: rims + 1]
    cos_ref, sin_ref = refs[rims + 1 : rims + 3]
    gq_ref, gkv_ref, bias_ref = refs[rims + 3 + late :]
    step = pl.program_id(0)
    set_bias(place, bias_ref, step)

    @pl.when(step == 0)
    def _():
        gkv_ref[...] = jnp.zeros_like(gkv_ref)

    head = query_ref.shape[1]
    scaling = head**-0.5
    keys = jnp.concatenate([ref[:, :head] for ref in table], axis=0)
    values = jnp.concatenate([ref[:, head:] for ref in table], axis=0)
    query, grad = query_ref[...], grad_ref[...]
    probs = softmax_rows(place, query, keys, bias_ref[...])
    grad_probs = dot_nt(grad, values)
    both = probs * grad_probs
    grad_scores = (both - probs * jnp.sum(both, axis=-1, keepdims=True)).astype(BF)
    grad_query = dot(grad_scores, keys) * scaling
    gq_ref[...] = turn(grad_query, cos_ref[...], -sin_ref[...]).astype(BF)
    gkv_ref[:, :head] += dot_tn(grad_scores, query) * scaling
    gkv_ref[:, head:] += dot_tn(probs.astype(BF), grad)


def out_kernel(shape, *refs):
    counts, seqs = shape
    slots, count, chunks = len(counts), sum(counts), max(counts)
    place, att_ref, rows_ref, gain_ref = refs[:4]
    mine = grouped(refs[4 : 4 + count], counts)
    theirs = grouped(refs[4 + count : 4 + 2 * count], counts)
    middle_ref, normed_ref, plain_ref = refs[4 + 2 * count :]
    seq, slot = place[0], place[1]
    model = rows_ref.shape[1]
    half = model // 2
    width = model // seqs
    left, right = att_ref[:, :half], att_ref[:, half:]
    for i in range(slots):
        total = piece_dot(left, mine[i]) + piece_dot(right, theirs[i])
        to = at(slot ^ i, total.shape[1])
        middle_ref[:, to] = rows_ref[:, to].astype(F32) + total
    scale = rms_of(middle_ref[...])
    for m in range(seqs):
        to = at(line_block(m, seq, seqs), width)
        gain = gain_ref[:, m * width : (m + 1) * width]
        normed_ref[:, to] = (middle_ref[:, to] * scale * gain).astype(BF)
        plain_ref[:, to] = att_ref[:, m * width : (m + 1) * width]


def mid_back_kernel(shape, *refs):
    counts, seqs = shape
    slots, count, chunks = len(counts), sum(counts), max(counts)
    place, grad_ref, middle_ref, cot_ref, gain_ref = refs[:5]
    mine = grouped(refs[5 : 5 + count], counts)
    theirs = grouped(refs[5 + count : 5 + 2 * count], counts)
    gmid_ref, gatt_ref, ggain_ref = refs[5 + 2 * count : 8 + 2 * count]
    branch = refs[8 + 2 * count :]
    seq, slot = place[0], place[1]
    model = middle_ref.shape[1]
    half = model // 2
    width = model // seqs
    scale = rms_of(middle_ref[...])
    mean = 0.0
    for m in range(seqs):
        to = at(line_block(m, seq, seqs), width)
        here = slice(m * width, (m + 1) * width)
        grad = grad_ref[:, to]
        unit = middle_ref[:, to] * scale
        ggain_ref[:, to] = jnp.sum(grad * unit, axis=0, keepdims=True)
        scaled = grad * gain_ref[:, here]
        gmid_ref[:, to] = scaled
        mean = mean + jnp.sum(scaled * unit, axis=1, keepdims=True)
    mean = mean * (1.0 / model)
    gmid_ref[...] = cot_ref[...].astype(F32) + scale * (
        gmid_ref[...] - middle_ref[...] * (scale * mean)
    )
    out_cols = model // slots
    for i in range(slots):
        branch[i][...] = gmid_ref[:, at(slot ^ i, out_cols)].astype(BF)
    for pieces, start in ((mine, 0), (theirs, half)):
        row = start
        for c in range(chunks):
            rows = half // chunks
            total = dot_nt(branch[0][...], chunk_of(pieces[0], c, chunks))
            for i in range(1, slots):
                total = total + dot_nt(branch[i][...], chunk_of(pieces[i], c, chunks))
            gatt_ref[:, row : row + rows] = total.astype(BF)
            row += rows


def input_back_kernel(shape, *refs):
    counts, seqs = shape
    slots, count, chunks = len(counts), sum(counts), max(counts)
    place, gq_ref, gkv_ref, rows_ref, gmid_ref, gain_ref = refs[:6]
    mine = grouped(refs[6 : 6 + count], counts)
    theirs = grouped(refs[6 + count : 6 + 2 * count], counts)
    kv_mine, kv_theirs = refs[6 + 2 * count : 8 + 2 * count]
    out_ref, ggain_ref, scaled_ref = refs[8 + 2 * count :]
    seq = place[0]
    model = rows_ref.shape[1]
    half = model // 2
    width = model // seqs
    cols = model // slots
    rows_in = rows_ref[...].astype(F32)
    scale = rms_of(rows_in)
    mean = 0.0
    for pieces, kv_ref, start in ((mine, kv_mine, 0), (theirs, kv_theirs, half)):
        row = 0
        for c in range(chunks):
            rows = half // chunks
            total = dot_nt(gkv_ref[...], kv_ref[row : row + rows])
            for i in range(slots):
                total = total + dot_nt(
                    gq_ref[:, i * cols : (i + 1) * cols], chunk_of(pieces[i], c, chunks)
                )
            for b in range(rows // width):
                m = (start + row) // width + b
                here = slice(m * width, (m + 1) * width)
                to = at(line_block(m, seq, seqs), width)
                grad = total[:, b * width : (b + 1) * width]
                unit = rows_ref[:, to].astype(F32) * scale
                ggain_ref[:, to] = jnp.sum(grad * unit, axis=0, keepdims=True)
                scaled = grad * gain_ref[:, here]
                scaled_ref[:, to] = scaled
                mean = mean + jnp.sum(scaled * unit, axis=1, keepdims=True)
            row += rows
    mean = mean * (1.0 / model)
    out_ref[...] = (
        gmid_ref[...] + scale * (scaled_ref[...] - rows_in * (scale * mean))
    ).astype(BF)


def share_kernel(slots, seqs, place, gate_ref, up_ref, out_ref):
    piece = gate_ref.shape[1] // (slots * seqs)
    width = piece * seqs
    for s in range(slots):

        @pl.when(place[1] == s)
        def _():
            for n, ref in enumerate((gate_ref, up_ref)):
                parts = [
                    ref[:, (q * slots + s) * piece : (q * slots + s + 1) * piece]
                    for q in range(seqs)
                ]
                out_ref[:, n * width : (n + 1) * width] = jnp.concatenate(parts, axis=1)


def parts_product(left, right):
    total, block, row = None, 0, 0
    for ref in left:
        rows = ref.shape[0]
        part = dot_tn(ref[...], right[block][row : row + rows])
        total = part if total is None else total + part
        row += rows
        if row == right[block].shape[0]:
            block, row = block + 1, 0
    return total


def line_grads_kernel(count, slots, place, *refs):
    normed, attended = refs[:count], refs[count : 2 * count]
    traded, branch = refs[2 * count : 2 * count + slots], refs[2 * count + slots :][:slots]
    gain_ref, out_ref = refs[2 * count + 2 * slots], refs[-1]
    first = parts_product(normed, traded)
    second = parts_product(attended, branch)
    start = first.shape[1]
    end = start + second.shape[1]
    out_ref[:, :start] = first.astype(BF)
    out_ref[:, start:end] = second.astype(BF)
    out_ref[:, end:] = gain_ref[...]


def cut_store(total, outs):
    row = 0
    for ref in outs:
        rows = ref.shape[0]
        ref[...] = total[row : row + rows].astype(BF)
        row += rows


def gate_kernel(count, *refs):
    tokens = refs[:count]
    wgate_ref, wup_ref, all_ref, gate_ref, up_ref, hidden_ref = refs[count:]

    @pl.when(pl.program_id(0) == 0)
    def _():
        row = 0
        for ref in tokens:
            all_ref[row : row + ref.shape[0]] = ref[...]
            row += ref.shape[0]

    tile = wgate_ref.shape[1]
    both = dot(all_ref[...], jnp.concatenate([wgate_ref[...], wup_ref[...]], axis=1))
    gate, up = both[:, :tile], both[:, tile:]
    gate_ref[...] = gate.astype(BF)
    up_ref[...] = up.astype(BF)
    hidden_ref[...] = (gate * jax.nn.sigmoid(gate) * up).astype(BF)


def rows_kernel(transposed, late, left_ref, right_ref, *refs):
    right = right_ref[...]
    total = dot_nt(left_ref[...], right) if transposed else dot(left_ref[...], right)
    cut_store(total, refs[late:])


def unline_kernel(seqs, place, *refs):
    out_ref = refs[seqs]
    for m in range(seqs):
        rows = refs[m].shape[0]
        to = pl.ds(pl.multiple_of(line_block(m, place[0], seqs) * rows, rows), rows)
        out_ref[to] = refs[m][...]


def unshare_kernel(slots, seqs, part_ref, gate_ref, up_ref):
    width = part_ref.shape[2] // 2
    piece = width // seqs
    for n, ref in enumerate((gate_ref, up_ref)):
        parts = [
            part_ref[s, :, n * width + q * piece : n * width + (q + 1) * piece]
            for q in range(seqs)
            for s in range(slots)
        ]
        ref[...] = jnp.concatenate(parts, axis=1).astype(F32)


def tie(value, *after):
    return pl.pallas_call(
        lambda *refs: None,
        out_shape=jax.ShapeDtypeStruct(value.shape, value.dtype),
        in_specs=[ANY] * (1 + len(after)),
        out_specs=ANY,
        input_output_aliases={0: 0},
    )(value, *after)


def fence(values, after):
    count = len(values)
    return list(
        pl.pallas_call(
            lambda *refs: None,
            out_shape=[jax.ShapeDtypeStruct(value.shape, value.dtype) for value in values],
            in_specs=[ANY] * (count + len(after)),
            out_specs=[ANY] * count,
            input_output_aliases={k: k for k in range(count)},
        )(*values, *after)
    )


class Flow:
    def __init__(self):
        self.now = []

    def at(self, *values):
        self.now = list(values)

    def go(self, *values):
        kept = {id(value) for value in values}
        return fence(list(values), [value for value in self.now if id(value) not in kept])


def call(kernel, inputs, late, out_shape, in_specs=None, scratch=()):
    count = len(inputs)
    single = not isinstance(out_shape, (tuple, list))

    def run(*refs):
        kernel(*refs[:count], *refs[count + len(late) :])

    return pl.pallas_call(
        run,
        out_shape=out_shape,
        in_specs=[SMEM] + [VMEM] * (count - 1) + [ANY] * len(late),
        out_specs=VMEM if single else (VMEM,) * len(out_shape),
        scratch_shapes=list(scratch),
        compiler_params=BIG,
    )(*inputs, *late)


def shape_of(rows, cols, kind):
    return jax.ShapeDtypeStruct((rows, cols), kind)


def shards(
    rows_in,
    lengths,
    norm1_gain,
    w_query,
    w_key,
    w_value,
    w_out,
    norm2_gain,
    w_gate,
    w_up,
    w_down,
    rows_cot,
    kv_cot,
):
    slots = lax.axis_size("slot")
    seqs = lax.axis_size("seq")
    slot = lax.axis_index("slot")
    seq = lax.axis_index("seq")
    tok_count = rows_in.shape[1]
    model = rows_in.shape[2]
    head_width = w_key.shape[1]
    head_count = w_query.shape[1] // head_width
    hop_count = WINDOW // tok_count
    key_count = WINDOW + tok_count
    rows_dev = w_query.shape[0]
    cols_slot = w_query.shape[1] // slots
    out_slot = w_out.shape[1] // slots
    hidden_all = w_gate.shape[1]
    piece = hidden_all // (slots * seqs)
    hidden_slot = piece * seqs
    half = model // 2
    extra = 16
    place = jnp.stack([seq, slot, lengths[0]]).astype(jnp.int32)
    rows_own, cot_own = rows_in[0], rows_cot[0]

    first_row = seq * tok_count
    query_pos = first_row + jnp.arange(tok_count, dtype=jnp.int32)
    row_valid = (query_pos < lengths[0]).astype(F32)[:, None]
    flow = Flow()

    gains = jnp.stack([norm1_gain, norm2_gain], axis=0)
    pack = jnp.concatenate(
        [lax.dynamic_slice_in_dim(w_query, slot * cols_slot, cols_slot, 1), w_key, w_value], axis=1
    )
    gains = jnp.pad(gains, ((0, extra - 2), (cols_slot, pack.shape[1] - cols_slot - rows_dev)))
    pack = jnp.concatenate([pack, gains], axis=0)
    pack_near = line_near(pack)
    cot_near = gather_near(cot_own * row_valid.astype(BF))
    gu_share = call(
        functools.partial(share_kernel, slots, seqs),
        (place, w_gate, w_up),
        (),
        shape_of(rows_dev, 2 * hidden_slot, BF),
    )
    out_share = lax.dynamic_slice_in_dim(w_out, slot * out_slot, out_slot, 1)
    down_share = lax.dynamic_slice_in_dim(w_down, slot * piece, piece, 0)
    flow.at(*pack_near[1:], *cot_near[1:], gu_share)

    *pack_near[1:], out_share = flow.go(*pack_near[1:], out_share)
    *cot_near[1:], down_share = flow.go(*cot_near[1:], down_share)
    pack_far = line_far(pack_near)
    out_near = line_near(out_share)
    cot_far = gather_far(cot_near)
    flow.at(*pack_far, *out_near[1:], *cot_far)

    pack_line = line_all(pack_near, pack_far)
    query_line = jnp.concatenate([block[:rows_dev, :cols_slot] for block in pack_line], axis=0)
    kv_gain = jnp.concatenate([block[:, cols_slot:] for block in pack_line], axis=0)
    query_line, kv_gain, out_near[-1], gu_share = flow.go(
        query_line, kv_gain, out_near[-1], gu_share
    )
    gu_w = lax.all_gather(gu_share, "seq", axis=0, tiled=True)
    down_w = lax.all_gather(down_share, "seq", axis=0, tiled=True)
    query_near = gather_near(query_line)
    query_other = [swap(query_line, "seq", 1)]
    kv_other = swap(kv_gain, "seq", 1)
    out_far = line_far(out_near)
    flow.at(*query_near[1:], query_other[0], kv_other, *out_far)

    query_near[1:] = flow.go(*query_near[1:])
    query_far = gather_far(query_near)
    query_other += [swap(part, "seq", 1) for part in query_near[1:]]
    flow.at(*query_far, *query_other[1:])

    *query_far, out_line = flow.go(
        *query_far, jnp.concatenate(line_all(out_near, out_far), axis=0)
    )
    query_other += [swap(part, "seq", 1) for part in query_far]
    query_w = query_near + query_far + query_other
    out_near = gather_near(out_line)
    flow.at(*query_w[len(query_near) :])
    kv_w, gain_line = [], []
    for part in (kv_gain, kv_other):
        part = part.reshape(seqs // 2, rows_dev + extra, -1)
        kv_w.append(part[:, :rows_dev].reshape(half, -1))
        gain_line.append(part[:, rows_dev : rows_dev + 2, :rows_dev])
    gain_line = jnp.concatenate(gain_line, axis=0).transpose(1, 0, 2).reshape(2, 1, model)
    gain_line = gain_line.astype(F32)
    gain_one, gain_two = gain_line[0], gain_line[1]
    shape = ((1, 1, 1, 2) if slots == 4 else (1,) * slots, seqs)

    cosine, sine = rope_tables(query_pos, head_width)
    cosine = jnp.concatenate([cosine, cosine], axis=1)
    sine = jnp.concatenate([-sine, sine], axis=1)
    normed, queries, shared = call(
        functools.partial(project_kernel, shape),
        (place, rows_own, gain_one, row_valid, cosine, sine, *query_w, *kv_w),
        (),
        (
            shape_of(tok_count, model, BF),
            shape_of(tok_count, head_count * head_width, BF),
            shape_of(tok_count, 2 * head_width, BF),
        ),
        scratch=[pltpu.VMEM((tok_count, model), BF)],
    )
    out_other = [swap(out_near[0], "seq", 1)]
    table = [shifted(shared, "seq", hop) for hop in range(hop_count, 0, -1)] + [shared]
    flow.at(*table[:-1], out_other[0], *out_near[1:])

    slot_heads = head_count // slots
    block_heads = rows_dev // head_width

    def own_col(p, place):
        return (0, p)

    def line_col(p, place):
        head = (place[1] ^ (p // slot_heads)) * slot_heads + p % slot_heads
        spot = line_place(head // block_heads, place[0], seqs)
        return (0, spot * block_heads + head % block_heads)

    def fixed(p, place):
        return (0, 0)

    head_own = pl.BlockSpec((tok_count, head_width), own_col)
    head_line = pl.BlockSpec((tok_count, head_width), line_col)
    table_spec = [pl.BlockSpec((tok_count, 2 * head_width), fixed)] * (hop_count + 1)
    angle_spec = [pl.BlockSpec((tok_count, head_width), fixed)] * 2
    bias_scratch = [pltpu.VMEM((tok_count, key_count), F32)]
    out_near[1:] = flow.go(*out_near[1:])
    out_far = gather_far(out_near)
    out_other += [swap(part, "seq", 1) for part in out_near[1:]]
    late = out_near[1:]
    attended = pl.pallas_call(
        functools.partial(attend_kernel, hop_count, len(late)),
        out_shape=shape_of(tok_count, head_count * head_width, BF),
        grid_spec=pltpu.PrefetchScalarGridSpec(
            num_scalar_prefetch=1,
            grid=(head_count,),
            in_specs=[head_own] + table_spec + [ANY] * len(late),
            out_specs=head_line,
            scratch_shapes=bias_scratch,
        ),
        compiler_params=BIG,
    )(place, queries, *table, *late)
    flow.at(*out_far, *out_other[1:], attended)
    if out_far:
        out_far = flow.go(*out_far)
    out_other += [swap(part, "seq", 1) for part in out_far]
    out_w = out_near + out_far + out_other
    middle, normed_two, attended = call(
        functools.partial(out_kernel, shape),
        (place, attended, rows_own, gain_two, *out_w),
        (),
        (
            shape_of(tok_count, model, F32),
            shape_of(tok_count, model, BF),
            shape_of(tok_count, model, BF),
        ),
    )

    normed_two_near = gather_near(normed_two)
    cot_rows = jnp.concatenate(cot_near + cot_far, axis=0)
    flow.at(*normed_two_near[1:], cot_rows)
    normed_two_near[1:] = flow.go(*normed_two_near[1:])
    normed_two_parts = normed_two_near + gather_far(normed_two_near)
    flow.at(*normed_two_parts[len(normed_two_near) - 1 :])

    normed_near = gather_near(tie(normed, *normed_two_parts[slots - 1 :]))
    tokens = slots * tok_count
    tile = 128
    if hidden_slot % tile == 0:
        steps = hidden_slot // tile
        part_spec = pl.BlockSpec((tokens, tile), lambda j: (0, j))
        normed_two_all, gate_out, up_out, hidden = pl.pallas_call(
            functools.partial(gate_kernel, len(normed_two_parts)),
            out_shape=(shape_of(tokens, model, BF),) + (shape_of(tokens, hidden_slot, BF),) * 3,
            grid=(steps,),
            in_specs=[pl.BlockSpec(part.shape, lambda j: (0, 0)) for part in normed_two_parts]
            + [
                pl.BlockSpec((model, tile), lambda j: (0, j)),
                pl.BlockSpec((model, tile), lambda j: (0, steps + j)),
            ],
            out_specs=(pl.BlockSpec((tokens, model), lambda j: (0, 0)),) + (part_spec,) * 3,
            compiler_params=BIG,
        )(*normed_two_parts, gu_w, gu_w)
        gate_out, up_out = gate_out.astype(F32), up_out.astype(F32)
    else:
        normed_two_all = jnp.concatenate(normed_two_parts, axis=0)
        gu_out = dot(normed_two_all, gu_w)
        gate_out, up_out = gu_out[:, :hidden_slot], gu_out[:, hidden_slot:]
        hidden = (gate_out * jax.nn.sigmoid(gate_out) * up_out).astype(BF)
    sig_gate = jax.nn.sigmoid(gate_out)
    cot_rows = tie(cot_rows, *normed_near[1:], hidden)
    grad_down = dot_tn(hidden, cot_rows).astype(BF)
    own_down = lax.psum_scatter(grad_down, "seq", scatter_dimension=0, tiled=True)
    *normed_near[1:], attended = fence([*normed_near[1:], attended], [cot_rows])
    normed_all = normed_near + gather_far(normed_near)
    attended_near = gather_near(attended)

    grad_hidden = dot_nt(cot_rows, down_w)
    grad_gate = grad_hidden * up_out * sig_gate * (1.0 + gate_out * (1.0 - sig_gate))
    grad_up = grad_hidden * gate_out * sig_gate
    grad_gu = jnp.concatenate([grad_gate.astype(BF), grad_up.astype(BF)], axis=1)
    grad_gate_w = dot_tn(normed_two_all, grad_gu[:, :hidden_slot]).astype(BF)
    grad_gu = tie(grad_gu, *normed_all[slots - 1 :], *attended_near[1:], grad_gate_w)
    half_tok = tok_count // 2
    cut_rows = [tok_count] + [half_tok] * 6 if slots == 4 else [tok_count] * slots

    def cut_product(left, right, transposed, late):
        width = 512
        depth = left.shape[1]
        right_spec = (
            pl.BlockSpec((width, depth), lambda j: (j, 0))
            if transposed
            else pl.BlockSpec((depth, width), lambda j: (0, j))
        )
        return list(
            pl.pallas_call(
                functools.partial(rows_kernel, transposed, len(late)),
                out_shape=[shape_of(rows, model, BF) for rows in cut_rows],
                grid=(model // width,),
                in_specs=[pl.BlockSpec(left.shape, lambda j: (0, 0)), right_spec]
                + [ANY] * len(late),
                out_specs=[pl.BlockSpec((rows, width), lambda j: (0, j)) for rows in cut_rows],
                compiler_params=BIG,
            )(left, right, *late)
        )

    attended_near[1:] = fence(attended_near[1:], [grad_gu])
    attended_all = attended_near + gather_far(attended_near)
    grad_parts = cut_product(grad_gu, gu_w, True, ())
    if slots == 4:
        grad_parts[5:] = fence(
            grad_parts[5:], attended_all[slots - 1 :]
        )
    passed = scatter_pass(grad_parts)
    down_parts = cut_product(tie(hidden, grad_parts[0]), down_w, False, ())
    if slots == 4:
        *passed, grad_parts[2], grad_parts[3], grad_gu = fence(
            [*passed, grad_parts[2], grad_parts[3], grad_gu], [down_parts[0]]
        )
    near = scatter_near(grad_parts)
    far = scatter_far(grad_parts, passed)
    grad_gate_w = tie(grad_gate_w, own_down, *passed)
    own_gate = lax.psum_scatter(grad_gate_w, "seq", scatter_dimension=0, tiled=True)
    grad_up_w = dot_tn(normed_two_all, grad_gu[:, hidden_slot:]).astype(BF)
    if slots == 4:
        near[0], near[1], far[0], far[1] = fence([*near, *far], [grad_up_w])
    grad_normed_two = scatter_total(grad_parts, near, far)
    down_parts[-1] = tie(down_parts[-1], grad_normed_two)
    down_passed = scatter_pass(
        [*down_parts[:-2], tie(down_parts[-2], down_parts[-1]), down_parts[-1]]
    )

    grad_middle, grad_attended, grad_gain_two, *branch = call(
        functools.partial(mid_back_kernel, shape),
        (place, grad_normed_two, middle, cot_own, gain_two, *out_w),
        (grad_up_w,),
        (
            shape_of(tok_count, model, F32),
            shape_of(tok_count, head_count * head_width, BF),
            shape_of(1, model, F32),
        )
        + (shape_of(tok_count, out_slot, BF),) * slots,
    )
    branch_all = trade_slot(branch)
    own_down_near = gather_near(tie(own_down, branch[0]))

    grad_query, grad_table = pl.pallas_call(
        functools.partial(attend_back_kernel, hop_count, 0),
        out_shape=(
            shape_of(tok_count, head_count * head_width, BF),
            shape_of(key_count, 2 * head_width, F32),
        ),
        grid_spec=pltpu.PrefetchScalarGridSpec(
            num_scalar_prefetch=1,
            grid=(head_count,),
            in_specs=[head_own, head_line] + table_spec + angle_spec,
            out_specs=(head_own, pl.BlockSpec((key_count, 2 * head_width), fixed)),
            scratch_shapes=bias_scratch,
        ),
        compiler_params=BIG,
    )(place, queries, grad_attended, *table, cosine, sine)
    grad_table, *down_passed = fence([grad_table, *down_passed], branch_all[1:])
    grad_up_w = tie(grad_up_w, own_gate, grad_table)
    own_up = lax.psum_scatter(grad_up_w, "seq", scatter_dimension=0, tiled=True)
    own_grad = grad_table[WINDOW:] + kv_cot[0].astype(F32)
    for hop in range(1, hop_count + 1):
        lower = (hop_count - hop) * tok_count
        own_grad = own_grad + shifted(
            grad_table[lower : lower + tok_count].astype(BF), "seq", -hop
        ).astype(F32)
    own_grad = own_grad * row_valid
    grad_key = own_grad[:, :head_width]
    grad_key = grad_key * cosine - jnp.roll(grad_key, head_width // 2, axis=1) * sine
    grad_kv = jnp.concatenate([grad_key, own_grad[:, head_width:]], axis=1).astype(BF)
    grad_kv, down_parts[2], *own_down_near[1:] = fence(
        [grad_kv, down_parts[2], *own_down_near[1:]], []
    )
    down_near = scatter_near(
        [*down_parts[:3], tie(down_parts[3], down_parts[2]), *down_parts[4:]]
        if slots == 4
        else down_parts
    )
    traded = [
        jnp.concatenate([grad_query[:, j * cols_slot : (j + 1) * cols_slot], grad_kv], axis=1)
        for j in range(slots)
    ]
    late = traded
    traded = trade_slot(traded)
    grad_inputs, grad_gain_one = call(
        functools.partial(input_back_kernel, shape),
        (place, grad_query, grad_kv, rows_own, grad_middle, gain_one, *query_w, *kv_w),
        late,
        (shape_of(tok_count, model, BF), shape_of(1, model, F32)),
        scratch=[pltpu.VMEM((tok_count, model), F32)],
    )
    gain_grads = jnp.concatenate([grad_gain_one, grad_gain_two], axis=0).astype(BF)
    gain_grads = jnp.pad(gain_grads.T, ((0, 0), (0, head_width - 2)))
    late = [grad_inputs, *traded[1:], *down_near]
    gain_grads, down_parts[1], *down_passed = fence(
        [gain_grads, down_parts[1], *down_passed], late
    )
    own_down_near[1:] = fence(own_down_near[1:], [gain_grads])
    down_far = scatter_far(down_parts, down_passed)
    own_down_all = own_down_near + gather_far(own_down_near)
    width_all = traded[0].shape[1] + branch_all[0].shape[1] + head_width
    places = seqs // 2

    def line_grads(start, late):
        def columns(m, place):
            return (0, line_block_at(start + m, place[0], seqs))

        def rows(m, place):
            return (line_block_at(start + m, place[0], seqs), 0)

        return pl.pallas_call(
            functools.partial(line_grads_kernel, len(normed_all), slots),
            out_shape=shape_of(half, width_all, BF),
            grid_spec=pltpu.PrefetchScalarGridSpec(
                num_scalar_prefetch=1,
                grid=(places,),
                in_specs=[
                    pl.BlockSpec((part.shape[0], rows_dev), columns)
                    for part in normed_all + attended_all
                ]
                + [pl.BlockSpec(part.shape, fixed) for part in traded + branch_all]
                + [pl.BlockSpec((rows_dev, head_width), rows)]
                + [ANY] * len(late),
                out_specs=pl.BlockSpec((rows_dev, width_all), lambda m, place: (m, 0)),
            ),
            compiler_params=BIG,
        )(place, *normed_all, *attended_all, *traded, *branch_all, gain_grads, *late)

    mine = line_grads(0, ())
    theirs = line_grads(places, (mine,))
    passed = swap(theirs, "seq", 1)
    line = line_sums(mine, passed)
    first = line_first(line)
    down_total = scatter_total(down_parts, down_near, down_far)
    result = (middle + down_total * row_valid).astype(BF)
    second = line_second(line, first)
    own_hidden = jnp.concatenate([own_gate, own_up], axis=1)
    hidden_parts = lax.all_gather(own_hidden, "slot", axis=0)
    own = line_total(line, first, second)
    kv_end = cols_slot + 2 * head_width
    shared_out = jnp.concatenate([own[:, :cols_slot], own[:, kv_end:]], axis=1).astype(BF)
    shared_near = gather_near(shared_out)
    row_tile = 32

    gate_grad, up_grad = pl.pallas_call(
        functools.partial(unshare_kernel, slots, seqs),
        out_shape=(shape_of(rows_dev, hidden_all, F32),) * 2,
        grid=(rows_dev // row_tile,),
        in_specs=[pl.BlockSpec((slots, row_tile, 2 * hidden_slot), lambda r: (0, r, 0))],
        out_specs=(pl.BlockSpec((row_tile, hidden_all), lambda r: (r, 0)),) * 2,
        compiler_params=BIG,
    )(hidden_parts)
    all_own = jnp.concatenate(shared_near + gather_far(shared_near), axis=0)
    all_own = all_own.reshape(slots, rows_dev, -1)
    all_own = jnp.stack(
        [lax.dynamic_index_in_dim(all_own, slot ^ j, 0, keepdims=False) for j in range(slots)]
    )

    def by_slot(parts):
        parts = jnp.concatenate(parts, axis=0).reshape(slots, -1, parts[0].shape[1])
        return jnp.stack(
            [lax.dynamic_index_in_dim(parts, slot ^ j, 0, keepdims=False) for j in range(slots)]
        )

    def slot_columns(parts):
        return parts.transpose(1, 0, 2).reshape(rows_dev, -1).astype(F32)

    query_grad = slot_columns(all_own[:, :, :cols_slot])
    out_grad_w = slot_columns(all_own[:, :, cols_slot : cols_slot + out_slot])
    gain_total = jnp.sum(all_own[:, :, cols_slot + out_slot :][:, :, :2].astype(F32), axis=0)
    down_grad = by_slot(own_down_all).reshape(slots * piece, model).astype(F32)
    return (
        result[None],
        shared[None],
        grad_inputs[None],
        gain_total[:, 0],
        query_grad,
        own[:, cols_slot : cols_slot + head_width].astype(F32),
        own[:, cols_slot + head_width : kv_end].astype(F32),
        out_grad_w,
        gain_total[:, 1],
        gate_grad,
        up_grad,
        down_grad,
    )


def solution(mesh):
    placed = (
        P("slot", "seq", None),
        P("slot"),
        P("seq"),
        P("seq", None),
        P("seq", None),
        P("seq", None),
        P("seq", None),
        P("seq"),
        P("seq", None),
        P("seq", None),
        P("seq", None),
        P("slot", "seq", None),
        P("slot", "seq", None),
    )
    return jax.shard_map(
        shards,
        mesh=mesh,
        in_specs=placed,
        out_specs=(
            P("slot", "seq", None),
            P("slot", "seq", None),
            P("slot", "seq", None),
            P("seq"),
            P("seq", None),
            P("seq", None),
            P("seq", None),
            P("seq", None),
            P("seq"),
            P("seq", None),
            P("seq", None),
            P("seq", None),
        ),
        check_vma=False,
    )
```
